32 devices in a mesh: gx: 4 (over z), gy: 4 (over y, x), gz: 2 (over core).
Axes of the slice: x: 2, y: 2, z: 4, core: 2. Of those that a mesh axis runs over, the one named last changes fastest.
Arguments:
- moment: bfloat16 [1024, 1024, 1024], P('gx', 'gy', 'gz'), may hold values from -0.625 to 0.625
- factor_start: bfloat16 [1024, 128], replicated, may hold values from -6 to 6
Outputs:
- factor_out: float32 [1024, 128], P('gx')
The draws below stay inside these ranges and needn't reach their ends.
All inputs are finite; a program needn't handle non-finite values.
Results may differ from the reference program's by a relative error of at most 0.0005.
Values may be sent and summed in bfloat16 or wider, within the bound.
A program may use at most 128 MiB of HBM per device.

```python
import jax
import jax.numpy as jnp
from jax import lax

N = 1024
R = 128
ITERS = 1
N_GZ = 2


def draw_moment(key, part):
    key = jax.random.fold_in(key, 11)
    noise_key, shared_key, block_key = jax.random.split(key, 3)
    position = jnp.arange(N, dtype=jnp.float32) / (N - 1)
    row_block = jnp.arange(N, dtype=jnp.int32) // 16
    block_draw = jax.random.uniform(block_key, (N // 16,), jnp.float32, 0.0, 1.0)
    shared = jnp.clip(jax.random.normal(shared_key, (N, N), jnp.float32), -2.0833, 2.0833)
    base = jnp.clip(jax.random.normal(noise_key, (N, N, N), jnp.float32), -6.0, 6.0)
    rise = jnp.exp(jnp.log(3.2) * position)
    jitter = jnp.exp(jnp.log(0.55) * block_draw)
    row_scale = rise * jitter[row_block]
    values = (0.7 * base + 0.3 * shared[None, :, :]) * N ** (-0.5) * row_scale[:, None, None]
    return values.astype(jnp.bfloat16)


def gaussian(rng, shape, width, most, held_as=jnp.bfloat16):
    array = jax.random.normal(rng, shape, jnp.float32) * width
    return jnp.minimum(jnp.maximum(array, -most), most).astype(held_as)


def setup_inputs(seed: int = 0) -> dict:
    key_of = jax.random.split(jax.random.key(seed), 3)
    return {
        "moment": draw_moment(jax.random.fold_in(key_of[2], 71), 0),
        "factor_start": gaussian(key_of[1], (N, R), 1.0, 6.0),
    }


def reference(moment, factor_start):
    kblk = N // N_GZ
    scale_n = 1.0 / N ** 0.5
    factor = factor_start
    blocks = moment.reshape(N // 32, 32, N, N)
    result = None
    for sweep in range(ITERS):

        def mode_block(block):
            acc = jnp.zeros((block.shape[0], N, R), jnp.float32)
            for part in range(N_GZ):
                piece = jnp.einsum('ijk,kb->ijb', block[:, :, part * kblk:(part + 1) * kblk].astype(jnp.float32), factor[part * kblk:(part + 1) * kblk].astype(jnp.float32))
                piece = lax.optimization_barrier(piece.astype(jnp.bfloat16))
                acc = acc + piece.astype(jnp.float32)
            ytens = acc.astype(jnp.bfloat16)
            ztens = jnp.einsum('ijb,ja->iba', ytens.astype(jnp.float32), factor.astype(jnp.float32)) * scale_n
            return ztens.astype(jnp.bfloat16)
        zfull = lax.map(mode_block, blocks).reshape(N, R, R)
        cgram = jnp.einsum('iba,ir->bar', zfull.astype(jnp.float32), factor.astype(jnp.float32)) * scale_n
        cgram = cgram.astype(jnp.bfloat16)
        vnew = jnp.einsum('iba,bar->ir', zfull.astype(jnp.float32), cgram.astype(jnp.float32)) / R
        total = jnp.sum(vnew * vnew)
        result = vnew * lax.rsqrt(total / (N * R) + 1e-06)
        factor = result.astype(jnp.bfloat16)
    return result
```

```python
import functools

import jax
import jax.numpy as jnp
from jax import lax
from jax.experimental import pallas as pl
from jax.experimental.pallas import tpu as pltpu
from jax.sharding import PartitionSpec as P

MESH = pl.DeviceIdType.MESH
F32 = jnp.float32
BF16 = jnp.bfloat16
STEP_ROWS = 16
MBUFS = 4
PIECES = 4


def sweep_kernel(nx, order, m_hbm, u_ref, out_ref, mbuf, uj_t, ui_t, zf, zsend, prx, kept, xs, rx, zz,
                 cs, crx, cown, lsend, r1, r2, cfull, vs, vrx, vfull, ss, ssrx,
                 m_sem, p_send, p_recv, x_send, x_recv, y_send, y_recv, c_send, c_recv, l_send, r1_recv, r2_recv,
                 o_send, g_send, g_recv, v_send, v_recv, f_send, f_recv, s_send, s_recv):
    rows_i, rows_j, rows_k = m_hbm.shape
    rank = u_ref.shape[1]
    steps = rows_i // STEP_ROWS
    scale = 1.0 / order**0.5
    me_x, me_y, me_c = lax.axis_index("gx"), lax.axis_index("gy"), lax.axis_index("gz")
    bit_x, bit_y = lax.rem(me_y, 2), lax.div(me_y, 2)
    at_x = (me_x, me_y + 1 - 2 * bit_x, me_c)
    at_y = (me_x, me_y + 2 - 4 * bit_y, me_c)
    at_c = (me_x, me_y, 1 - me_c)
    me_e = me_y * 2 + me_c
    half = rank // 2
    quarter = rank // 4
    part = rank // 8
    sub = rank // 16
    piece = sub // 2

    def group(d):
        e = lax.rem(me_e + d, 8)
        return e, (me_x, lax.div(e, 2), lax.rem(e, 2))

    def line(d):
        return (lax.rem(me_x + d, nx), me_y, me_c)

    def m_copy(t):
        slot = lax.rem(t, MBUFS)
        return pltpu.make_async_copy(m_hbm.at[pl.ds(t * STEP_ROWS, STEP_ROWS)], mbuf.at[slot], m_sem.at[slot])

    def remote(src, dst, send, recv, to):
        return pltpu.make_async_remote_copy(src_ref=src, dst_ref=dst, send_sem=send, recv_sem=recv,
                                            device_id=to, device_id_type=MESH)

    for t in range(MBUFS - 1):
        m_copy(t).start()

    barrier = pltpu.get_barrier_semaphore()
    for d in range(1, 8):
        pl.semaphore_signal(barrier, inc=1, device_id=group(d)[1], device_id_type=MESH)
    for d in range(1, nx):
        pl.semaphore_signal(barrier, inc=1, device_id=line(d), device_id_type=MESH)

    uj_t[...] = u_ref[pl.ds(me_y * rows_j, rows_j), :].astype(F32).T.astype(BF16)
    ui_t[...] = u_ref[pl.ds(me_x * rows_i, rows_i), :].astype(F32).T.astype(BF16)
    pl.semaphore_wait(barrier, 7 + nx - 1)

    def p_copy(t):
        return remote(zsend.at[t], prx.at[t], p_send.at[t], p_recv.at[t], at_c)

    def x_copy(t):
        return remote(xs.at[t, pl.ds(0, part)], rx.at[t, pl.ds(0, part)], x_send.at[t], x_recv.at[t], at_x)

    def y_copy(t):
        return remote(xs.at[t, pl.ds(part, part)], rx.at[t, pl.ds(part, part)], y_send.at[t], y_recv.at[t], at_y)

    def contract(t):
        par = lax.rem(t, 2)
        m_copy(t).wait()
        block = mbuf[lax.rem(t, MBUFS)].reshape(STEP_ROWS * rows_j, rows_k)
        uk = u_ref[pl.ds(me_c * rows_k, rows_k), :]
        y = jnp.dot(block, uk, preferred_element_type=F32).astype(BF16)
        for i in range(0, STEP_ROWS, 2):
            pair = jnp.concatenate([y[i * rows_j:(i + 1) * rows_j], y[(i + 1) * rows_j:(i + 2) * rows_j]], axis=1)
            z = jnp.dot(uj_t[...], pair, preferred_element_type=F32) * scale
            zf[par, pl.ds(i, rank, stride=STEP_ROWS), :] = z[:, :rank]
            zf[par, pl.ds(i + 1, rank, stride=STEP_ROWS), :] = z[:, rank:]
        other = zf[par, pl.ds((1 - me_c) * half * STEP_ROWS, half * STEP_ROWS), :]
        zsend[t] = other.astype(BF16).reshape(half, STEP_ROWS, rank)
        p_copy(t).start()

    def pair_sum(t):
        par = lax.rem(t, 2)
        p_copy(t).wait_recv()

        def summed(first):
            mine = zf[par, pl.ds((me_c * half + first) * STEP_ROWS, part * STEP_ROWS), :]
            return mine.reshape(part, STEP_ROWS, rank) + prx[t, pl.ds(first, part)].astype(F32)

        xs[t, pl.ds(0, part)] = summed((1 - bit_x) * part).astype(BF16)
        x_copy(t).start()
        xs[t, pl.ds(part, part)] = summed(quarter + (1 - bit_y) * part).astype(BF16)
        y_copy(t).start()
        kept[t, pl.ds(0, part)] = summed(bit_x * part)
        kept[t, pl.ds(part, part)] = summed(quarter + bit_y * part)

    contract(0)

    def body(t, carry):
        @pl.when(t + MBUFS - 2 < steps)
        def _():
            m_copy(t + MBUFS - 2).start()

        pair_sum(t - 1)
        contract(t)
        return carry

    lax.fori_loop(1, steps, body, 0)
    pair_sum(steps - 1)

    def landed(t, carry):
        x_copy(t).wait_recv()
        y_copy(t).wait_recv()
        return carry

    lax.fori_loop(0, steps, landed, 0)

    def total_z(a, carry):
        zz[a] = (kept[:, a] + rx[:, a].astype(F32)).astype(BF16).reshape(rows_i, rank)
        return carry

    lax.fori_loop(0, 2 * part, total_z, 0)

    def first_of(k, mine):
        if k % 2 == 0:
            bit = bit_y if mine else 1 - bit_y
            return bit * sub + (k // 2) * piece
        bit = bit_x if mine else 1 - bit_x
        return part + bit * sub + (k // 2) * piece

    def wide_z(first):
        return jnp.concatenate([zz[first + n] for n in range(piece)], axis=1)

    def core_part(first):
        return jnp.dot(ui_t[...], wide_z(first), preferred_element_type=F32) * scale

    def c_copy(k):
        return remote(cs.at[k], crx.at[k], c_send.at[k], c_recv.at[k], at_y if k % 2 == 0 else at_x)

    for k in range(PIECES):
        c = core_part(first_of(k, False))
        for n in range(piece):
            cs[k, n] = c[:, n * rank:(n + 1) * rank].astype(BF16)
        c_copy(k).start()
    for k in range(PIECES):
        c = core_part(first_of(k, True))
        for n in range(piece):
            cown[k, n] = c[:, n * rank:(n + 1) * rank]

    mid = nx // 2
    side = lax.div(me_x, mid)
    inward = (me_x + 1 - 2 * side, me_y, me_c)
    outward = (me_x - 1 + 2 * side, me_y, me_c)
    inner = jnp.logical_or(me_x == mid - 1, me_x == mid)
    has_out = jnp.logical_and(me_x > 0, me_x < nx - 1)
    not_inner = jnp.logical_not(inner)

    def l1_copy(k):
        return remote(lsend.at[k], r1.at[k], l_send.at[k], r1_recv.at[k], inward)

    def l2_copy(k):
        return remote(lsend.at[k], r2.at[k], l_send.at[k], r2_recv.at[k], inward)

    def o_copy(k):
        return remote(cfull.at[pl.ds(first_of(k, True), piece)], r2.at[k], o_send.at[k], r2_recv.at[k], outward)

    def g_copy(k):
        here = cfull.at[pl.ds(first_of(k, True), piece)]
        return remote(here, here, g_send.at[k], g_recv.at[k], at_y if k % 2 == 0 else at_x)

    def g_landed(k):
        here = cfull.at[pl.ds(first_of(k, False), piece)]
        return remote(here, here, g_send.at[k], g_recv.at[k], at_y if k % 2 == 0 else at_x)

    for k in range(PIECES):
        c_copy(k).wait_recv()
        cown[k] = cown[k] + crx[k].astype(F32)

        @pl.when(has_out)
        def _():
            l1_copy(k).wait_recv()
            cown[k] = cown[k] + r1[k].astype(F32)

        lsend[k] = cown[k].astype(BF16)

        @pl.when(inner)
        def _():
            l2_copy(k).start()

        @pl.when(not_inner)
        def _():
            l1_copy(k).start()

    def v_part(first):
        c = jnp.concatenate([cfull[first + n] for n in range(piece)], axis=1)
        return lax.dot_general(wide_z(first), c, (((1,), (1,)), ((), ())), preferred_element_type=F32)

    for k in range(PIECES):
        l2_copy(k).wait_recv()
        first = first_of(k, True)

        @pl.when(inner)
        def _():
            cfull[pl.ds(first, piece)] = (lsend[k].astype(F32) + r2[k].astype(F32)).astype(BF16)

        @pl.when(not_inner)
        def _():
            cfull[pl.ds(first, piece)] = r2[k]

        @pl.when(has_out)
        def _():
            o_copy(k).start()

        g_copy(k).start()
        if k == 0:
            vs[...] = v_part(first)
        else:
            vs[...] = vs[...] + v_part(first)
    for k in range(PIECES):
        g_landed(k).wait_recv()
        vs[...] = vs[...] + v_part(first_of(k, False))

    vrows = rows_i // 8

    def v_copy(d):
        e, to = group(d)
        return remote(vs.at[pl.ds(e * vrows, vrows)], vrx.at[d - 1], v_send.at[d - 1], v_recv.at[d - 1], to)

    def f_copy(d):
        here = vfull.at[pl.ds(me_e * vrows, vrows)]
        return remote(here, here, f_send.at[d - 1], f_recv.at[d - 1], group(d)[1])

    def f_landed(d):
        here = vfull.at[pl.ds(group(8 - d)[0] * vrows, vrows)]
        return remote(here, here, f_send.at[d - 1], f_recv.at[d - 1], group(d)[1])

    def s_copy(d):
        return remote(ss, ssrx.at[d - 1], s_send.at[d - 1], s_recv.at[d - 1], line(d))

    for d in range(1, 8):
        v_copy(d).start()
    total = vs[pl.ds(me_e * vrows, vrows), :]
    for d in range(1, 8):
        v_copy(d).wait_recv()
        total = total + vrx[d - 1]
    vfull[pl.ds(me_e * vrows, vrows), :] = total * (1.0 / rank)
    for d in range(1, 8):
        f_copy(d).start()
    for d in range(1, 8):
        f_landed(d).wait_recv()
    vnew = vfull[...]
    ss[...] = jnp.sum((vnew * vnew).reshape(rows_i // 8, 8, rank), axis=0)
    for d in range(1, nx):
        s_copy(d).start()
    square = ss[...]
    for d in range(1, nx):
        s_copy(d).wait_recv()
        square = square + ssrx[d - 1]
    square = jnp.sum(jnp.sum(square, axis=0, keepdims=True), axis=1, keepdims=True)
    out_ref[...] = vnew * lax.rsqrt(square / (order * rank) + 1e-06)

    def sent(t, carry):
        p_copy(t).wait_send()
        x_copy(t).wait_send()
        y_copy(t).wait_send()
        return carry

    lax.fori_loop(0, steps, sent, 0)
    for k in range(PIECES):
        c_copy(k).wait_send()
        l2_copy(k).wait_send()
        g_copy(k).wait_send()

        @pl.when(has_out)
        def _():
            o_copy(k).wait_send()
    for d in range(1, 8):
        v_copy(d).wait_send()
        f_copy(d).wait_send()
    for d in range(1, nx):
        s_copy(d).wait_send()


def fused(nx, moment, factor_start):
    rows_i, rows_j, rows_k = moment.shape
    order, rank = factor_start.shape
    steps = rows_i // STEP_ROWS
    half, part, piece = rank // 2, rank // 8, rank // 32
    vrows = rows_i // 8
    vmem, dma = pltpu.VMEM, pltpu.SemaphoreType.DMA
    scratch = [
        vmem((MBUFS, STEP_ROWS, rows_j, rows_k), BF16),
        vmem((rank, rows_j), BF16),
        vmem((rank, rows_i), BF16),
        vmem((2, rank * STEP_ROWS, rank), F32),
        vmem((steps, half, STEP_ROWS, rank), BF16),
        vmem((steps, half, STEP_ROWS, rank), BF16),
        vmem((steps, 2 * part, STEP_ROWS, rank), F32),
        vmem((steps, 2 * part, STEP_ROWS, rank), BF16),
        vmem((steps, 2 * part, STEP_ROWS, rank), BF16),
        vmem((2 * part, rows_i, rank), BF16),
        vmem((PIECES, piece, rank, rank), BF16),
        vmem((PIECES, piece, rank, rank), BF16),
        vmem((PIECES, piece, rank, rank), F32),
        vmem((PIECES, piece, rank, rank), BF16),
        vmem((PIECES, piece, rank, rank), BF16),
        vmem((PIECES, piece, rank, rank), BF16),
        vmem((2 * part, rank, rank), BF16),
        vmem((rows_i, rank), F32),
        vmem((7, vrows, rank), F32),
        vmem((rows_i, rank), F32),
        vmem((8, rank), F32),
        vmem((nx - 1, 8, rank), F32),
        dma((MBUFS,)),
        dma((steps,)), dma((steps,)), dma((steps,)), dma((steps,)), dma((steps,)), dma((steps,)),
        dma((PIECES,)), dma((PIECES,)), dma((PIECES,)), dma((PIECES,)), dma((PIECES,)),
        dma((PIECES,)), dma((PIECES,)), dma((PIECES,)),
        dma((7,)), dma((7,)), dma((7,)), dma((7,)),
        dma((nx - 1,)), dma((nx - 1,)),
    ]
    return pl.pallas_call(
        functools.partial(sweep_kernel, nx, order),
        out_shape=jax.ShapeDtypeStruct((rows_i, rank), F32),
        in_specs=[pl.BlockSpec(memory_space=pl.ANY), pl.BlockSpec(memory_space=pltpu.VMEM)],
        out_specs=pl.BlockSpec(memory_space=pltpu.VMEM),
        scratch_shapes=scratch,
        compiler_params=pltpu.CompilerParams(collective_id=0, has_side_effects=True,
                                             vmem_limit_bytes=60 * 1024 * 1024),
        cost_estimate=pl.CostEstimate(flops=2 * rows_i * rows_j * rank * (rows_k + rank),
                                      bytes_accessed=2 * rows_i * rows_j * rows_k, transcendentals=0),
    )(moment, factor_start)


def plain(moment, factor_start):
    rows_i, rows_j, rows_k = moment.shape
    order, rank = factor_start.shape
    scale = 1.0 / order**0.5
    krows = lax.dynamic_slice_in_dim(factor_start, lax.axis_index("gz") * rows_k, rows_k, 0)
    jrows = lax.dynamic_slice_in_dim(factor_start, lax.axis_index("gy") * rows_j, rows_j, 0)
    irows = lax.dynamic_slice_in_dim(factor_start, lax.axis_index("gx") * rows_i, rows_i, 0)
    y = jnp.einsum("ijk,kb->ijb", moment, krows, preferred_element_type=F32).astype(BF16)
    z = jnp.einsum("ijb,ja->iba", y, jrows, preferred_element_type=F32) * scale
    z = lax.psum_scatter(z, "gz", scatter_dimension=1, tiled=True)
    z = lax.psum_scatter(z, "gy", scatter_dimension=2, tiled=True).astype(BF16)
    c = lax.psum(jnp.einsum("iba,ir->bar", z, irows, preferred_element_type=F32), "gx")
    c = (c * scale).astype(BF16)
    v = lax.psum(jnp.einsum("iba,bar->ir", z, c, preferred_element_type=F32), ("gy", "gz")) / rank
    total = lax.psum(jnp.sum(v * v), "gx")
    return v * lax.rsqrt(total / (order * rank) + 1e-06)


def solution(mesh):
    nx, ny, nz = mesh.shape["gx"], mesh.shape["gy"], mesh.shape["gz"]

    def local(moment, factor_start):
        rows_i, rank = moment.shape[0], factor_start.shape[1]
        if ny == 4 and nz == 2 and nx % 2 == 0 and rank == 128 and rows_i % 128 == 0:
            return fused(nx, moment, factor_start)
        return plain(moment, factor_start)

    return jax.shard_map(local, mesh=mesh, in_specs=(P("gx", "gy", "gz"), P()), out_specs=P("gx", None),
                         check_vma=False)
```

```python
import functools

import jax
import jax.numpy as jnp
from jax import lax
from jax.experimental import pallas as pl
from jax.experimental.pallas import tpu as pltpu
from jax.sharding import PartitionSpec as P

MESH = pl.DeviceIdType.MESH
F32 = jnp.float32
BF16 = jnp.bfloat16
STEP_ROWS = 16
MBUFS = 4
PIECES = 8
LAG = 4
AHEAD = 2


def sweep_kernel(nx, order, m_hbm, u_ref, out_ref, mbuf, vs_t, uj_t, ui_t, zown, zsend, prx, xs, ys, rxx, rxy, zz,
                 cs, crx, cown, lsend, r1, r2, cfull, vs, vrx, vfull, ss, ssrx,
                 m_sem, p_send, p_recv, x_send, x_recv, y_send, y_recv, c_send, c_recv, l_send, r1_recv, r2_recv,
                 o_send, g_send, g_recv, v_send, v_recv, f_send, f_recv, s_send, s_recv):
    rows_i, rows_j, rows_k = m_hbm.shape
    rank = u_ref.shape[1]
    steps = rows_i // STEP_ROWS
    scale = 1.0 / order**0.5
    me_x, me_y, me_c = lax.axis_index("gx"), lax.axis_index("gy"), lax.axis_index("gz")
    bit_x, bit_y = lax.rem(me_y, 2), lax.div(me_y, 2)
    at_x = (me_x, me_y + 1 - 2 * bit_x, me_c)
    at_y = (me_x, me_y + 2 - 4 * bit_y, me_c)
    at_c = (me_x, me_y, 1 - me_c)
    me_e = me_y * 2 + me_c
    half = rank // 2
    quarter = rank // 4
    part = rank // 8
    sub = rank // 16
    piece = 2 * sub // PIECES

    def group(d):
        e = lax.rem(me_e + d, 8)
        return e, (me_x, lax.div(e, 2), lax.rem(e, 2))

    def line(d):
        return (lax.rem(me_x + d, nx), me_y, me_c)

    def m_copy(t):
        slot = lax.rem(t, MBUFS)
        return pltpu.make_async_copy(m_hbm.at[pl.ds(t * STEP_ROWS, STEP_ROWS)], mbuf.at[slot], m_sem.at[slot])

    def remote(src, dst, send, recv, to):
        return pltpu.make_async_remote_copy(src_ref=src, dst_ref=dst, send_sem=send, recv_sem=recv,
                                            device_id=to, device_id_type=MESH)

    for t in range(MBUFS - 1):
        m_copy(t).start()

    barrier = pltpu.get_barrier_semaphore()
    for d in range(1, 8):
        pl.semaphore_signal(barrier, inc=1, device_id=group(d)[1], device_id_type=MESH)
    for d in range(1, nx):
        pl.semaphore_signal(barrier, inc=1, device_id=line(d), device_id_type=MESH)

    uj = u_ref[pl.ds(me_y * rows_j, rows_j), :].astype(F32).T
    vs_t[...] = uj.astype(BF16)
    for n, core in enumerate((me_c, 1 - me_c)):
        for m, first in enumerate((bit_x * part, quarter + bit_y * part,
                                   (1 - bit_x) * part, quarter + (1 - bit_y) * part)):
            uj_t[pl.ds(n * half + m * part, part), :] = vs_t[pl.ds(core * half + first, part), :]
    ui_t[...] = u_ref[pl.ds(me_x * rows_i, rows_i), :].astype(F32).T.astype(BF16)
    pl.semaphore_wait(barrier, 7 + nx - 1)

    def p_copy(t):
        return remote(zsend.at[t], prx.at[t], p_send.at[t], p_recv.at[t], at_c)

    def x_copy(t):
        return remote(xs.at[t], rxx.at[t], x_send.at[t], x_recv.at[t], at_x)

    def y_copy(t):
        return remote(ys.at[t], rxy.at[t], y_send.at[t], y_recv.at[t], at_y)

    def contract(t):
        m_copy(t).wait()
        block = mbuf[lax.rem(t, MBUFS)].reshape(STEP_ROWS * rows_j, rows_k)
        uk = u_ref[pl.ds(me_c * rows_k, rows_k), :]
        y = jnp.dot(block, uk, preferred_element_type=F32).astype(BF16)
        for i in range(0, STEP_ROWS, 2):
            pair = jnp.concatenate([y[i * rows_j:(i + 1) * rows_j], y[(i + 1) * rows_j:(i + 2) * rows_j]], axis=1)
            z = jnp.dot(uj_t[...], pair, preferred_element_type=F32) * scale
            for n in range(2):
                zown[t, i + n] = z[:half, n * rank:(n + 1) * rank]
                zsend[t, i + n] = z[half:, n * rank:(n + 1) * rank].astype(BF16)
        p_copy(t).start()

    def pair_sum(t):
        p_copy(t).wait_recv()
        xs[t] = (zown[t, :, pl.ds(2 * part, part)] + prx[t, :, pl.ds(2 * part, part)].astype(F32)).astype(BF16)
        x_copy(t).start()
        ys[t] = (zown[t, :, pl.ds(3 * part, part)] + prx[t, :, pl.ds(3 * part, part)].astype(F32)).astype(BF16)
        y_copy(t).start()

    def land(t):
        x_copy(t).wait_recv()
        y_copy(t).wait_recv()
        for i in range(STEP_ROWS):
            both = zown[t, i, pl.ds(0, 2 * part)] + prx[t, i, pl.ds(0, 2 * part)].astype(F32)
            far = jnp.concatenate([rxx[t, i], rxy[t, i]], axis=0).astype(F32)
            zz[pl.ds(t * STEP_ROWS + i, 2 * part, stride=rows_i), :] = both + far

    def fetch(t):
        @pl.when(t + MBUFS - 2 < steps)
        def _():
            m_copy(t + MBUFS - 2).start()

    def early(t, carry):
        fetch(t)
        pair_sum(t - 1)
        contract(t)
        return carry

    def body(t, carry):
        fetch(t)
        pair_sum(t - 1)
        land(t - LAG)
        contract(t)
        return carry

    contract(0)
    lax.fori_loop(1, LAG, early, 0)
    lax.fori_loop(LAG, steps, body, 0)
    pair_sum(steps - 1)

    def late(t, carry):
        land(t)
        return carry

    lax.fori_loop(steps - LAG, steps, late, 0)

    def first_of(k, mine):
        if k % 2 == 0:
            bit = bit_y if mine else 1 - bit_y
            return bit * sub + (k // 2) * piece
        bit = bit_x if mine else 1 - bit_x
        return part + bit * sub + (k // 2) * piece

    def wide_z(first):
        return jnp.concatenate([zz[pl.ds((first + n) * rows_i, rows_i), :].astype(BF16) for n in range(piece)], axis=1)

    def core_part(first):
        return jnp.dot(ui_t[...], wide_z(first), preferred_element_type=F32) * scale

    def c_copy(k):
        return remote(cs.at[k], crx.at[k], c_send.at[k], c_recv.at[k], at_y if k % 2 == 0 else at_x)

    for k in range(PIECES):
        c = core_part(first_of(k, False))
        for n in range(piece):
            cs[k, n] = c[:, n * rank:(n + 1) * rank].astype(BF16)
        c_copy(k).start()
    mid = nx // 2
    side = lax.div(me_x, mid)
    inward = (me_x + 1 - 2 * side, me_y, me_c)
    outward = (me_x - 1 + 2 * side, me_y, me_c)
    inner = jnp.logical_or(me_x == mid - 1, me_x == mid)
    has_out = jnp.logical_and(me_x > 0, me_x < nx - 1)
    not_inner = jnp.logical_not(inner)

    def l1_copy(k):
        return remote(lsend.at[k], r1.at[k], l_send.at[k], r1_recv.at[k], inward)

    def l2_copy(k):
        return remote(lsend.at[k], r2.at[k], l_send.at[k], r2_recv.at[k], inward)

    def o_copy(k):
        return remote(cfull.at[pl.ds(first_of(k, True), piece)], r2.at[k], o_send.at[k], r2_recv.at[k], outward)

    def g_copy(k):
        here = cfull.at[pl.ds(first_of(k, True), piece)]
        return remote(here, here, g_send.at[k], g_recv.at[k], at_y if k % 2 == 0 else at_x)

    def g_landed(k):
        here = cfull.at[pl.ds(first_of(k, False), piece)]
        return remote(here, here, g_send.at[k], g_recv.at[k], at_y if k % 2 == 0 else at_x)

    def to_middle(k):
        c = core_part(first_of(k, True))
        c_copy(k).wait_recv()
        for n in range(piece):
            cown[k, n] = c[:, n * rank:(n + 1) * rank] + crx[k, n].astype(F32)

        @pl.when(has_out)
        def _():
            l1_copy(k).wait_recv()
            cown[k] = cown[k] + r1[k].astype(F32)

        lsend[k] = cown[k].astype(BF16)

        @pl.when(inner)
        def _():
            l2_copy(k).start()

        @pl.when(not_inner)
        def _():
            l1_copy(k).start()

    def v_part(first):
        c = jnp.concatenate([cfull[first + n] for n in range(piece)], axis=1)
        return lax.dot_general(wide_z(first), c, (((1,), (1,)), ((), ())), preferred_element_type=F32)

    def from_middle(k):
        l2_copy(k).wait_recv()
        first = first_of(k, True)

        @pl.when(inner)
        def _():
            cfull[pl.ds(first, piece)] = (lsend[k].astype(F32) + r2[k].astype(F32)).astype(BF16)

        @pl.when(not_inner)
        def _():
            cfull[pl.ds(first, piece)] = r2[k]

        @pl.when(has_out)
        def _():
            o_copy(k).start()

        g_copy(k).start()
        if k == 0:
            vs[...] = v_part(first)
        else:
            vs[...] = vs[...] + v_part(first)

    for k in range(PIECES + AHEAD):
        if k < PIECES:
            to_middle(k)
        if k >= AHEAD:
            from_middle(k - AHEAD)
    for k in range(PIECES):
        g_landed(k).wait_recv()
        vs[...] = vs[...] + v_part(first_of(k, False))

    vrows = rows_i // 8

    def v_copy(d):
        e, to = group(d)
        return remote(vs.at[pl.ds(e * vrows, vrows)], vrx.at[d - 1], v_send.at[d - 1], v_recv.at[d - 1], to)

    def f_copy(d):
        here = vfull.at[pl.ds(me_e * vrows, vrows)]
        return remote(here, here, f_send.at[d - 1], f_recv.at[d - 1], group(d)[1])

    def f_landed(d):
        here = vfull.at[pl.ds(group(8 - d)[0] * vrows, vrows)]
        return remote(here, here, f_send.at[d - 1], f_recv.at[d - 1], group(d)[1])

    def s_copy(d):
        return remote(ss, ssrx.at[d - 1], s_send.at[d - 1], s_recv.at[d - 1], line(d))

    for d in range(1, 8):
        v_copy(d).start()
    total = vs[pl.ds(me_e * vrows, vrows), :]
    for d in range(1, 8):
        v_copy(d).wait_recv()
        total = total + vrx[d - 1]
    vfull[pl.ds(me_e * vrows, vrows), :] = total * (1.0 / rank)
    for d in range(1, 8):
        f_copy(d).start()
    for d in range(1, 8):
        f_landed(d).wait_recv()
    vnew = vfull[...]
    ss[...] = jnp.sum((vnew * vnew).reshape(rows_i // 8, 8, rank), axis=0)
    for d in range(1, nx):
        s_copy(d).start()
    square = ss[...]
    for d in range(1, nx):
        s_copy(d).wait_recv()
        square = square + ssrx[d - 1]
    square = jnp.sum(jnp.sum(square, axis=0, keepdims=True), axis=1, keepdims=True)
    out_ref[...] = vnew * lax.rsqrt(square / (order * rank) + 1e-06)

    def sent(t, carry):
        p_copy(t).wait_send()
        x_copy(t).wait_send()
        y_copy(t).wait_send()
        return carry

    lax.fori_loop(0, steps, sent, 0)
    for k in range(PIECES):
        c_copy(k).wait_send()
        l2_copy(k).wait_send()
        g_copy(k).wait_send()

        @pl.when(has_out)
        def _():
            o_copy(k).wait_send()
    for d in range(1, 8):
        v_copy(d).wait_send()
        f_copy(d).wait_send()
    for d in range(1, nx):
        s_copy(d).wait_send()


def fused(nx, moment, factor_start):
    rows_i, rows_j, rows_k = moment.shape
    order, rank = factor_start.shape
    steps = rows_i // STEP_ROWS
    half, part, piece = rank // 2, rank // 8, rank // 64
    vrows = rows_i // 8
    vmem, dma = pltpu.VMEM, pltpu.SemaphoreType.DMA
    scratch = [
        vmem((MBUFS, STEP_ROWS, rows_j, rows_k), BF16),
        vmem((rank, rows_j), BF16),
        vmem((rank, rows_j), BF16),
        vmem((rank, rows_i), BF16),
        vmem((steps, STEP_ROWS, half, rank), F32),
        vmem((steps, STEP_ROWS, half, rank), BF16),
        vmem((steps, STEP_ROWS, half, rank), BF16),
        vmem((steps, STEP_ROWS, part, rank), BF16),
        vmem((steps, STEP_ROWS, part, rank), BF16),
        vmem((steps, STEP_ROWS, part, rank), BF16),
        vmem((steps, STEP_ROWS, part, rank), BF16),
        vmem((2 * part * rows_i, rank), F32),
        vmem((PIECES, piece, rank, rank), BF16),
        vmem((PIECES, piece, rank, rank), BF16),
        vmem((PIECES, piece, rank, rank), F32),
        vmem((PIECES, piece, rank, rank), BF16),
        vmem((PIECES, piece, rank, rank), BF16),
        vmem((PIECES, piece, rank, rank), BF16),
        vmem((2 * part, rank, rank), BF16),
        vmem((rows_i, rank), F32),
        vmem((7, vrows, rank), F32),
        vmem((rows_i, rank), F32),
        vmem((8, rank), F32),
        vmem((nx - 1, 8, rank), F32),
        dma((MBUFS,)),
        dma((steps,)), dma((steps,)), dma((steps,)), dma((steps,)), dma((steps,)), dma((steps,)),
        dma((PIECES,)), dma((PIECES,)), dma((PIECES,)), dma((PIECES,)), dma((PIECES,)),
        dma((PIECES,)), dma((PIECES,)), dma((PIECES,)),
        dma((7,)), dma((7,)), dma((7,)), dma((7,)),
        dma((nx - 1,)), dma((nx - 1,)),
    ]
    return pl.pallas_call(
        functools.partial(sweep_kernel, nx, order),
        out_shape=jax.ShapeDtypeStruct((rows_i, rank), F32),
        in_specs=[pl.BlockSpec(memory_space=pl.ANY), pl.BlockSpec(memory_space=pltpu.VMEM)],
        out_specs=pl.BlockSpec(memory_space=pltpu.VMEM),
        scratch_shapes=scratch,
        compiler_params=pltpu.CompilerParams(collective_id=0, has_side_effects=True,
                                             vmem_limit_bytes=60 * 1024 * 1024),
        cost_estimate=pl.CostEstimate(flops=2 * rows_i * rows_j * rank * (rows_k + rank),
                                      bytes_accessed=2 * rows_i * rows_j * rows_k, transcendentals=0),
    )(moment, factor_start)


def plain(moment, factor_start):
    rows_i, rows_j, rows_k = moment.shape
    order, rank = factor_start.shape
    scale = 1.0 / order**0.5
    krows = lax.dynamic_slice_in_dim(factor_start, lax.axis_index("gz") * rows_k, rows_k, 0)
    jrows = lax.dynamic_slice_in_dim(factor_start, lax.axis_index("gy") * rows_j, rows_j, 0)
    irows = lax.dynamic_slice_in_dim(factor_start, lax.axis_index("gx") * rows_i, rows_i, 0)
    y = jnp.einsum("ijk,kb->ijb", moment, krows, preferred_element_type=F32).astype(BF16)
    z = jnp.einsum("ijb,ja->iba", y, jrows, preferred_element_type=F32) * scale
    z = lax.psum_scatter(z, "gz", scatter_dimension=1, tiled=True)
    z = lax.psum_scatter(z, "gy", scatter_dimension=2, tiled=True).astype(BF16)
    c = lax.psum(jnp.einsum("iba,ir->bar", z, irows, preferred_element_type=F32), "gx")
    c = (c * scale).astype(BF16)
    v = lax.psum(jnp.einsum("iba,bar->ir", z, c, preferred_element_type=F32), ("gy", "gz")) / rank
    total = lax.psum(jnp.sum(v * v), "gx")
    return v * lax.rsqrt(total / (order * rank) + 1e-06)


def solution(mesh):
    nx, ny, nz = mesh.shape["gx"], mesh.shape["gy"], mesh.shape["gz"]

    def local(moment, factor_start):
        rows_i, rank = moment.shape[0], factor_start.shape[1]
        if ny == 4 and nz == 2 and nx % 2 == 0 and rank == 128 and rows_i % 128 == 0:
            return fused(nx, moment, factor_start)
        return plain(moment, factor_start)

    return jax.shard_map(local, mesh=mesh, in_specs=(P("gx", "gy", "gz"), P()), out_specs=P("gx", None),
                         check_vma=False)
```

```python
import functools

import jax
import jax.numpy as jnp
from jax import lax
from jax.experimental import pallas as pl
from jax.experimental.pallas import tpu as pltpu
from jax.sharding import PartitionSpec as P

MESH = pl.DeviceIdType.MESH
F32 = jnp.float32
BF16 = jnp.bfloat16
STEP_ROWS = 16
MBUFS = 4
PIECES = 8
LAG = 4
AHEAD = 2


def sweep_kernel(nx, order, m_hbm, u_ref, out_ref, mbuf, vs_t, uj_t, ui_t, zown, zsend, prx, xs, ys, rxx, rxy, zz,
                 cs, crx, cown, lsend, r1, r2, cfull, vs, vrx, vfull, ss, ssrx,
                 m_sem, p_send, p_recv, x_send, x_recv, y_send, y_recv, c_send, c_recv, l_send, r1_recv, r2_recv,
                 o_send, g_send, g_recv, v_send, v_recv, f_send, f_recv, s_send, s_recv):
    rows_i, rows_j, rows_k = m_hbm.shape
    rank = u_ref.shape[1]
    steps = rows_i // STEP_ROWS
    scale = 1.0 / order**0.5
    me_x, me_y, me_c = lax.axis_index("gx"), lax.axis_index("gy"), lax.axis_index("gz")
    bit_x, bit_y = lax.rem(me_y, 2), lax.div(me_y, 2)
    at_x = (me_x, me_y + 1 - 2 * bit_x, me_c)
    at_y = (me_x, me_y + 2 - 4 * bit_y, me_c)
    at_c = (me_x, me_y, 1 - me_c)
    me_e = me_y * 2 + me_c
    half = rank // 2
    quarter = rank // 4
    part = rank // 8
    sub = rank // 16
    piece = 2 * sub // PIECES

    def group(d):
        e = lax.rem(me_e + d, 8)
        return e, (me_x, lax.div(e, 2), lax.rem(e, 2))

    def line(d):
        return (lax.rem(me_x + d, nx), me_y, me_c)

    def m_copy(t):
        slot = lax.rem(t, MBUFS)
        return pltpu.make_async_copy(m_hbm.at[pl.ds(t * STEP_ROWS, STEP_ROWS)], mbuf.at[slot], m_sem.at[slot])

    def remote(src, dst, send, recv, to):
        return pltpu.make_async_remote_copy(src_ref=src, dst_ref=dst, send_sem=send, recv_sem=recv,
                                            device_id=to, device_id_type=MESH)

    for t in range(MBUFS - 1):
        m_copy(t).start()

    barrier = pltpu.get_barrier_semaphore()
    for d in range(1, 8):
        pl.semaphore_signal(barrier, inc=1, device_id=group(d)[1], device_id_type=MESH)
    for d in range(1, nx):
        pl.semaphore_signal(barrier, inc=1, device_id=line(d), device_id_type=MESH)

    uj = u_ref[pl.ds(me_y * rows_j, rows_j), :].astype(F32).T
    vs_t[...] = uj.astype(BF16)
    for n, core in enumerate((me_c, 1 - me_c)):
        for m, first in enumerate((bit_x * part, quarter + bit_y * part,
                                   (1 - bit_x) * part, quarter + (1 - bit_y) * part)):
            uj_t[pl.ds(n * half + m * part, part), :] = vs_t[pl.ds(core * half + first, part), :]
    ui_t[...] = u_ref[pl.ds(me_x * rows_i, rows_i), :].astype(F32).T.astype(BF16)
    pl.semaphore_wait(barrier, 7 + nx - 1)

    def p_copy(t):
        return remote(zsend.at[t], prx.at[t], p_send.at[t], p_recv.at[t], at_c)

    def x_copy(t):
        return remote(xs.at[t], rxx.at[t], x_send.at[t], x_recv.at[t], at_x)

    def y_copy(t):
        return remote(ys.at[t], rxy.at[t], y_send.at[t], y_recv.at[t], at_y)

    def contract(t):
        m_copy(t).wait()
        block = mbuf[lax.rem(t, MBUFS)].reshape(STEP_ROWS * rows_j, rows_k)
        uk = u_ref[pl.ds(me_c * rows_k, rows_k), :]
        y = jnp.dot(block, uk, preferred_element_type=F32).astype(BF16)
        for i in range(0, STEP_ROWS, 2):
            pair = jnp.concatenate([y[i * rows_j:(i + 1) * rows_j], y[(i + 1) * rows_j:(i + 2) * rows_j]], axis=1)
            z = jnp.dot(uj_t[...], pair, preferred_element_type=F32) * scale
            for n in range(2):
                zown[t, i + n] = z[:half, n * rank:(n + 1) * rank]
                zsend[t, i + n] = z[half:, n * rank:(n + 1) * rank].astype(BF16)
        p_copy(t).start()

    def pair_sum(t):
        p_copy(t).wait_recv()
        xs[t] = (zown[t, :, pl.ds(2 * part, part)] + prx[t, :, pl.ds(2 * part, part)].astype(F32)).astype(BF16)
        x_copy(t).start()
        ys[t] = (zown[t, :, pl.ds(3 * part, part)] + prx[t, :, pl.ds(3 * part, part)].astype(F32)).astype(BF16)
        y_copy(t).start()

    def land(t):
        x_copy(t).wait_recv()
        y_copy(t).wait_recv()
        for i in range(STEP_ROWS):
            both = zown[t, i, pl.ds(0, 2 * part)] + prx[t, i, pl.ds(0, 2 * part)].astype(F32)
            far = jnp.concatenate([rxx[t, i], rxy[t, i]], axis=0).astype(F32)
            zz[pl.ds(t * STEP_ROWS + i, 2 * part, stride=rows_i), :] = both + far

    def fetch(t):
        @pl.when(t + MBUFS - 2 < steps)
        def _():
            m_copy(t + MBUFS - 2).start()

    def early(t, carry):
        fetch(t)
        pair_sum(t - 1)
        contract(t)
        return carry

    def body(t, carry):
        fetch(t)
        pair_sum(t - 1)
        land(t - LAG)
        contract(t)
        return carry

    contract(0)
    lax.fori_loop(1, LAG, early, 0)
    lax.fori_loop(LAG, steps, body, 0)
    pair_sum(steps - 1)

    def late(t, carry):
        land(t)
        return carry

    lax.fori_loop(steps - LAG, steps, late, 0)

    def first_of(k, mine):
        if k % 2 == 0:
            bit = bit_y if mine else 1 - bit_y
            return bit * sub + (k // 2) * piece
        bit = bit_x if mine else 1 - bit_x
        return part + bit * sub + (k // 2) * piece

    def wide_z(first):
        return jnp.concatenate([zz[pl.ds((first + n) * rows_i, rows_i), :].astype(BF16) for n in range(piece)], axis=1)

    def core_part(first):
        return jnp.dot(ui_t[...], wide_z(first), preferred_element_type=F32) * scale

    def c_copy(k):
        return remote(cs.at[k], crx.at[k], c_send.at[k], c_recv.at[k], at_y if k % 2 == 0 else at_x)

    for k in range(PIECES):
        c = core_part(first_of(k, False))
        for n in range(piece):
            cs[k, n] = c[:, n * rank:(n + 1) * rank].astype(BF16)
        c_copy(k).start()
    mid = nx // 2
    side = lax.div(me_x, mid)
    inward = (me_x + 1 - 2 * side, me_y, me_c)
    outward = (me_x - 1 + 2 * side, me_y, me_c)
    inner = jnp.logical_or(me_x == mid - 1, me_x == mid)
    has_out = jnp.logical_and(me_x > 0, me_x < nx - 1)
    not_inner = jnp.logical_not(inner)

    def l1_copy(k):
        return remote(lsend.at[k], r1.at[k], l_send.at[k], r1_recv.at[k], inward)

    def l2_copy(k):
        return remote(lsend.at[k], r2.at[k], l_send.at[k], r2_recv.at[k], inward)

    def o_copy(k):
        return remote(cfull.at[pl.ds(first_of(k, True), piece)], r2.at[k], o_send.at[k], r2_recv.at[k], outward)

    def g_copy(k):
        here = cfull.at[pl.ds(first_of(k, True), piece)]
        return remote(here, here, g_send.at[k], g_recv.at[k], at_y if k % 2 == 0 else at_x)

    def g_landed(k):
        here = cfull.at[pl.ds(first_of(k, False), piece)]
        return remote(here, here, g_send.at[k], g_recv.at[k], at_y if k % 2 == 0 else at_x)

    def own_sum(k):
        c = core_part(first_of(k, True))
        c_copy(k).wait_recv()
        for n in range(piece):
            cown[k, n] = c[:, n * rank:(n + 1) * rank] + crx[k, n].astype(F32)

    def add_outer(k):
        @pl.when(has_out)
        def _():
            l1_copy(k).wait_recv()
            cown[k] = cown[k] + r1[k].astype(F32)

        lsend[k] = cown[k].astype(BF16)

    def v_part(first):
        c = jnp.concatenate([cfull[first + n] for n in range(piece)], axis=1)
        return lax.dot_general(wide_z(first), c, (((1,), (1,)), ((), ())), preferred_element_type=F32)

    def send_back(k):
        @pl.when(has_out)
        def _():
            o_copy(k).start()

        g_copy(k).start()

    def add_v(k):
        part_v = v_part(first_of(k, True))
        vs[...] = part_v if k == 0 else vs[...] + part_v

    @pl.when(not_inner)
    def _():
        for k in range(PIECES):
            own_sum(k)
            add_outer(k)
            l1_copy(k).start()
        for k in range(PIECES):
            l2_copy(k).wait_recv()
            cfull[pl.ds(first_of(k, True), piece)] = r2[k]
            send_back(k)
            add_v(k)

    @pl.when(inner)
    def _():
        for k in range(PIECES + AHEAD):
            if k < PIECES:
                own_sum(k)
                add_outer(k)
                l2_copy(k).start()
            if k >= AHEAD:
                n = k - AHEAD
                l2_copy(n).wait_recv()
                cfull[pl.ds(first_of(n, True), piece)] = (lsend[n].astype(F32) + r2[n].astype(F32)).astype(BF16)
                send_back(n)
                add_v(n)

    for k in range(PIECES):
        g_landed(k).wait_recv()
        vs[...] = vs[...] + v_part(first_of(k, False))

    vrows = rows_i // 8

    def v_copy(d):
        e, to = group(d)
        return remote(vs.at[pl.ds(e * vrows, vrows)], vrx.at[d - 1], v_send.at[d - 1], v_recv.at[d - 1], to)

    def f_copy(d):
        here = vfull.at[pl.ds(me_e * vrows, vrows)]
        return remote(here, here, f_send.at[d - 1], f_recv.at[d - 1], group(d)[1])

    def f_landed(d):
        here = vfull.at[pl.ds(group(8 - d)[0] * vrows, vrows)]
        return remote(here, here, f_send.at[d - 1], f_recv.at[d - 1], group(d)[1])

    def s_copy(d):
        return remote(ss, ssrx.at[d - 1], s_send.at[d - 1], s_recv.at[d - 1], line(d))

    for d in range(1, 8):
        v_copy(d).start()
    total = vs[pl.ds(me_e * vrows, vrows), :]
    for d in range(1, 8):
        v_copy(d).wait_recv()
        total = total + vrx[d - 1]
    vfull[pl.ds(me_e * vrows, vrows), :] = total * (1.0 / rank)
    for d in range(1, 8):
        f_copy(d).start()
    for d in range(1, 8):
        f_landed(d).wait_recv()
    vnew = vfull[...]
    ss[...] = jnp.sum((vnew * vnew).reshape(rows_i // 8, 8, rank), axis=0)
    for d in range(1, nx):
        s_copy(d).start()
    square = ss[...]
    for d in range(1, nx):
        s_copy(d).wait_recv()
        square = square + ssrx[d - 1]
    square = jnp.sum(jnp.sum(square, axis=0, keepdims=True), axis=1, keepdims=True)
    out_ref[...] = vnew * lax.rsqrt(square / (order * rank) + 1e-06)

    def sent(t, carry):
        p_copy(t).wait_send()
        x_copy(t).wait_send()
        y_copy(t).wait_send()
        return carry

    lax.fori_loop(0, steps, sent, 0)
    for k in range(PIECES):
        c_copy(k).wait_send()
        l2_copy(k).wait_send()
        g_copy(k).wait_send()

        @pl.when(has_out)
        def _():
            o_copy(k).wait_send()
    for d in range(1, 8):
        v_copy(d).wait_send()
        f_copy(d).wait_send()
    for d in range(1, nx):
        s_copy(d).wait_send()


def fused(nx, moment, factor_start):
    rows_i, rows_j, rows_k = moment.shape
    order, rank = factor_start.shape
    steps = rows_i // STEP_ROWS
    half, part, piece = rank // 2, rank // 8, rank // 64
    vrows = rows_i // 8
    vmem, dma = pltpu.VMEM, pltpu.SemaphoreType.DMA
    scratch = [
        vmem((MBUFS, STEP_ROWS, rows_j, rows_k), BF16),
        vmem((rank, rows_j), BF16),
        vmem((rank, rows_j), BF16),
        vmem((rank, rows_i), BF16),
        vmem((steps, STEP_ROWS, half, rank), F32),
        vmem((steps, STEP_ROWS, half, rank), BF16),
        vmem((steps, STEP_ROWS, half, rank), BF16),
        vmem((steps, STEP_ROWS, part, rank), BF16),
        vmem((steps, STEP_ROWS, part, rank), BF16),
        vmem((steps, STEP_ROWS, part, rank), BF16),
        vmem((steps, STEP_ROWS, part, rank), BF16),
        vmem((2 * part * rows_i, rank), F32),
        vmem((PIECES, piece, rank, rank), BF16),
        vmem((PIECES, piece, rank, rank), BF16),
        vmem((PIECES, piece, rank, rank), F32),
        vmem((PIECES, piece, rank, rank), BF16),
        vmem((PIECES, piece, rank, rank), BF16),
        vmem((PIECES, piece, rank, rank), BF16),
        vmem((2 * part, rank, rank), BF16),
        vmem((rows_i, rank), F32),
        vmem((7, vrows, rank), F32),
        vmem((rows_i, rank), F32),
        vmem((8, rank), F32),
        vmem((nx - 1, 8, rank), F32),
        dma((MBUFS,)),
        dma((steps,)), dma((steps,)), dma((steps,)), dma((steps,)), dma((steps,)), dma((steps,)),
        dma((PIECES,)), dma((PIECES,)), dma((PIECES,)), dma((PIECES,)), dma((PIECES,)),
        dma((PIECES,)), dma((PIECES,)), dma((PIECES,)),
        dma((7,)), dma((7,)), dma((7,)), dma((7,)),
        dma((nx - 1,)), dma((nx - 1,)),
    ]
    return pl.pallas_call(
        functools.partial(sweep_kernel, nx, order),
        out_shape=jax.ShapeDtypeStruct((rows_i, rank), F32),
        in_specs=[pl.BlockSpec(memory_space=pl.ANY), pl.BlockSpec(memory_space=pltpu.VMEM)],
        out_specs=pl.BlockSpec(memory_space=pltpu.VMEM),
        scratch_shapes=scratch,
        compiler_params=pltpu.CompilerParams(collective_id=0, has_side_effects=True,
                                             vmem_limit_bytes=60 * 1024 * 1024),
        cost_estimate=pl.CostEstimate(flops=2 * rows_i * rows_j * rank * (rows_k + rank),
                                      bytes_accessed=2 * rows_i * rows_j * rows_k, transcendentals=0),
    )(moment, factor_start)


def plain(moment, factor_start):
    rows_i, rows_j, rows_k = moment.shape
    order, rank = factor_start.shape
    scale = 1.0 / order**0.5
    krows = lax.dynamic_slice_in_dim(factor_start, lax.axis_index("gz") * rows_k, rows_k, 0)
    jrows = lax.dynamic_slice_in_dim(factor_start, lax.axis_index("gy") * rows_j, rows_j, 0)
    irows = lax.dynamic_slice_in_dim(factor_start, lax.axis_index("gx") * rows_i, rows_i, 0)
    y = jnp.einsum("ijk,kb->ijb", moment, krows, preferred_element_type=F32).astype(BF16)
    z = jnp.einsum("ijb,ja->iba", y, jrows, preferred_element_type=F32) * scale
    z = lax.psum_scatter(z, "gz", scatter_dimension=1, tiled=True)
    z = lax.psum_scatter(z, "gy", scatter_dimension=2, tiled=True).astype(BF16)
    c = lax.psum(jnp.einsum("iba,ir->bar", z, irows, preferred_element_type=F32), "gx")
    c = (c * scale).astype(BF16)
    v = lax.psum(jnp.einsum("iba,bar->ir", z, c, preferred_element_type=F32), ("gy", "gz")) / rank
    total = lax.psum(jnp.sum(v * v), "gx")
    return v * lax.rsqrt(total / (order * rank) + 1e-06)


def solution(mesh):
    nx, ny, nz = mesh.shape["gx"], mesh.shape["gy"], mesh.shape["gz"]

    def local(moment, factor_start):
        rows_i, rank = moment.shape[0], factor_start.shape[1]
        if ny == 4 and nz == 2 and nx % 2 == 0 and rank == 128 and rows_i % 128 == 0:
            return fused(nx, moment, factor_start)
        return plain(moment, factor_start)

    return jax.shard_map(local, mesh=mesh, in_specs=(P("gx", "gy", "gz"), P()), out_specs=P("gx", None),
                         check_vma=False)
```

```python
import functools

import jax
import jax.numpy as jnp
from jax import lax
from jax.experimental import pallas as pl
from jax.experimental.pallas import tpu as pltpu
from jax.sharding import PartitionSpec as P

MESH = pl.DeviceIdType.MESH
F32 = jnp.float32
BF16 = jnp.bfloat16
STEP_ROWS = 16
MBUFS = 4
PIECES = 8
LAG = 4
AHEAD = 2


def sweep_kernel(nx, order, m_hbm, u_ref, out_ref, mbuf, vs_t, uk_t, ui_t, zown, zsend, prx, xs, ys, rxx, rxy, zz,
                 cs, crx, cown, lsend, r1, r2, cfull, vs, vrx, vfull, ss, ssrx,
                 m_sem, p_send, p_recv, x_send, x_recv, y_send, y_recv, c_send, c_recv, l_send, r1_recv, r2_recv,
                 o_send, g_send, g_recv, v_send, v_recv, f_send, f_recv, s_send, s_recv):
    rows_i, rows_j, rows_k = m_hbm.shape
    rank = u_ref.shape[1]
    steps = rows_i // STEP_ROWS
    scale = 1.0 / order**0.5
    me_x, me_y, me_c = lax.axis_index("gx"), lax.axis_index("gy"), lax.axis_index("gz")
    bit_x, bit_y = lax.rem(me_y, 2), lax.div(me_y, 2)
    at_x = (me_x, me_y + 1 - 2 * bit_x, me_c)
    at_y = (me_x, me_y + 2 - 4 * bit_y, me_c)
    at_c = (me_x, me_y, 1 - me_c)
    me_e = me_y * 2 + me_c
    half = rank // 2
    quarter = rank // 4
    part = rank // 8
    sub = rank // 16
    piece = 2 * sub // PIECES

    def group(d):
        e = lax.rem(me_e + d, 8)
        return e, (me_x, lax.div(e, 2), lax.rem(e, 2))

    def line(d):
        return (lax.rem(me_x + d, nx), me_y, me_c)

    def m_copy(t):
        slot = lax.rem(t, MBUFS)
        return pltpu.make_async_copy(m_hbm.at[pl.ds(t * STEP_ROWS, STEP_ROWS)], mbuf.at[slot], m_sem.at[slot])

    def remote(src, dst, send, recv, to):
        return pltpu.make_async_remote_copy(src_ref=src, dst_ref=dst, send_sem=send, recv_sem=recv,
                                            device_id=to, device_id_type=MESH)

    for t in range(MBUFS - 1):
        m_copy(t).start()

    barrier = pltpu.get_barrier_semaphore()
    for d in range(1, 8):
        pl.semaphore_signal(barrier, inc=1, device_id=group(d)[1], device_id_type=MESH)
    for d in range(1, nx):
        pl.semaphore_signal(barrier, inc=1, device_id=line(d), device_id_type=MESH)

    vs_t[...] = u_ref[pl.ds(me_c * rows_k, rows_k), :].astype(F32).T.astype(BF16)
    for n, core in enumerate((me_c, 1 - me_c)):
        for m, first in enumerate((bit_x * part, quarter + bit_y * part,
                                   (1 - bit_x) * part, quarter + (1 - bit_y) * part)):
            uk_t[pl.ds(n * half + m * part, part), :] = vs_t[pl.ds(core * half + first, part), :]
    ui_t[...] = u_ref[pl.ds(me_x * rows_i, rows_i), :].astype(F32).T.astype(BF16)
    pl.semaphore_wait(barrier, 7 + nx - 1)

    def p_copy(t):
        return remote(zsend.at[t], prx.at[t], p_send.at[t], p_recv.at[t], at_c)

    def x_copy(t):
        return remote(xs.at[t], rxx.at[t], x_send.at[t], x_recv.at[t], at_x)

    def y_copy(t):
        return remote(ys.at[t], rxy.at[t], y_send.at[t], y_recv.at[t], at_y)

    def contract(t):
        uj = u_ref[pl.ds(me_y * rows_j, rows_j), :]
        slot = lax.rem(t, MBUFS)
        for i in range(STEP_ROWS):
            y = lax.dot_general(uk_t[...], mbuf[slot, i], (((1,), (1,)), ((), ())), preferred_element_type=F32)
            z = jnp.dot(y.astype(BF16), uj, preferred_element_type=F32) * scale
            zown[t, i] = z[:half]
            zsend[t, i] = z[half:].astype(BF16)

    def pair_sum(t):
        xs[t] = (zown[t, :, pl.ds(2 * part, part)] + prx[t, :, pl.ds(2 * part, part)].astype(F32)).astype(BF16)
        ys[t] = (zown[t, :, pl.ds(3 * part, part)] + prx[t, :, pl.ds(3 * part, part)].astype(F32)).astype(BF16)

    def land(t):
        for i in range(STEP_ROWS):
            both = zown[t, i, pl.ds(0, 2 * part)] + prx[t, i, pl.ds(0, 2 * part)].astype(F32)
            far = jnp.concatenate([rxx[t, i], rxy[t, i]], axis=0).astype(F32)
            zz[pl.ds(t * STEP_ROWS + i, 2 * part, stride=rows_i), :] = both + far

    def await_pair(t):
        p_copy(t).wait_recv()

    def await_far(t):
        x_copy(t).wait_recv()
        y_copy(t).wait_recv()

    def send_far(t):
        x_copy(t).start()
        y_copy(t).start()

    def fetch(t):
        @pl.when(t + MBUFS - 2 < steps)
        def _():
            m_copy(t + MBUFS - 2).start()

    def early(t, carry):
        fetch(t)
        await_pair(t - 1)
        m_copy(t).wait()
        pair_sum(t - 1)
        send_far(t - 1)
        contract(t)
        p_copy(t).start()
        return carry

    def body(t, carry):
        fetch(t)
        await_pair(t - 1)
        await_far(t - LAG)
        m_copy(t).wait()
        pair_sum(t - 1)
        send_far(t - 1)
        land(t - LAG)
        contract(t)
        p_copy(t).start()
        return carry

    m_copy(0).wait()
    contract(0)
    p_copy(0).start()
    lax.fori_loop(1, LAG, early, 0)
    lax.fori_loop(LAG, steps, body, 0)
    await_pair(steps - 1)
    pair_sum(steps - 1)
    send_far(steps - 1)

    def late(t, carry):
        await_far(t)
        land(t)
        return carry

    lax.fori_loop(steps - LAG, steps, late, 0)

    def first_of(k, mine):
        if k % 2 == 0:
            bit = bit_y if mine else 1 - bit_y
            return bit * sub + (k // 2) * piece
        bit = bit_x if mine else 1 - bit_x
        return part + bit * sub + (k // 2) * piece

    def wide_z(first):
        return jnp.concatenate([zz[pl.ds((first + n) * rows_i, rows_i), :].astype(BF16) for n in range(piece)], axis=1)

    def core_part(first):
        return jnp.dot(ui_t[...], wide_z(first), preferred_element_type=F32) * scale

    def c_copy(k):
        return remote(cs.at[k], crx.at[k], c_send.at[k], c_recv.at[k], at_y if k % 2 == 0 else at_x)

    for k in range(PIECES):
        c = core_part(first_of(k, False))
        for n in range(piece):
            cs[k, n] = c[:, n * rank:(n + 1) * rank].astype(BF16)
        c_copy(k).start()
    mid = nx // 2
    side = lax.div(me_x, mid)
    inward = (me_x + 1 - 2 * side, me_y, me_c)
    outward = (me_x - 1 + 2 * side, me_y, me_c)
    inner = jnp.logical_or(me_x == mid - 1, me_x == mid)
    has_out = jnp.logical_and(me_x > 0, me_x < nx - 1)
    not_inner = jnp.logical_not(inner)

    def l1_copy(k):
        return remote(lsend.at[k], r1.at[k], l_send.at[k], r1_recv.at[k], inward)

    def l2_copy(k):
        return remote(lsend.at[k], r2.at[k], l_send.at[k], r2_recv.at[k], inward)

    def o_copy(k):
        return remote(cfull.at[pl.ds(first_of(k, True), piece)], r2.at[k], o_send.at[k], r2_recv.at[k], outward)

    def g_copy(k):
        here = cfull.at[pl.ds(first_of(k, True), piece)]
        return remote(here, here, g_send.at[k], g_recv.at[k], at_y if k % 2 == 0 else at_x)

    def g_landed(k):
        here = cfull.at[pl.ds(first_of(k, False), piece)]
        return remote(here, here, g_send.at[k], g_recv.at[k], at_y if k % 2 == 0 else at_x)

    def own_sum(k):
        c = core_part(first_of(k, True))
        c_copy(k).wait_recv()
        for n in range(piece):
            cown[k, n] = c[:, n * rank:(n + 1) * rank] + crx[k, n].astype(F32)

    def add_outer(k):
        @pl.when(has_out)
        def _():
            l1_copy(k).wait_recv()
            cown[k] = cown[k] + r1[k].astype(F32)

        lsend[k] = cown[k].astype(BF16)

    def v_part(first):
        c = jnp.concatenate([cfull[first + n] for n in range(piece)], axis=1)
        return lax.dot_general(wide_z(first), c, (((1,), (1,)), ((), ())), preferred_element_type=F32)

    def send_back(k):
        @pl.when(has_out)
        def _():
            o_copy(k).start()

        g_copy(k).start()

    def add_v(k):
        part_v = v_part(first_of(k, True))
        vs[...] = part_v if k == 0 else vs[...] + part_v

    @pl.when(not_inner)
    def _():
        for k in range(PIECES):
            own_sum(k)
            add_outer(k)
            l1_copy(k).start()
        for k in range(PIECES):
            l2_copy(k).wait_recv()
            cfull[pl.ds(first_of(k, True), piece)] = r2[k]
            send_back(k)
            add_v(k)

    @pl.when(inner)
    def _():
        for k in range(PIECES + AHEAD):
            if k < PIECES:
                own_sum(k)
                add_outer(k)
                l2_copy(k).start()
            if k >= AHEAD:
                n = k - AHEAD
                l2_copy(n).wait_recv()
                cfull[pl.ds(first_of(n, True), piece)] = (lsend[n].astype(F32) + r2[n].astype(F32)).astype(BF16)
                send_back(n)
                add_v(n)

    for k in range(PIECES):
        g_landed(k).wait_recv()
        vs[...] = vs[...] + v_part(first_of(k, False))

    vrows = rows_i // 8

    def v_copy(d):
        e, to = group(d)
        return remote(vs.at[pl.ds(e * vrows, vrows)], vrx.at[d - 1], v_send.at[d - 1], v_recv.at[d - 1], to)

    def f_copy(d):
        here = vfull.at[pl.ds(me_e * vrows, vrows)]
        return remote(here, here, f_send.at[d - 1], f_recv.at[d - 1], group(d)[1])

    def f_landed(d):
        here = vfull.at[pl.ds(group(8 - d)[0] * vrows, vrows)]
        return remote(here, here, f_send.at[d - 1], f_recv.at[d - 1], group(d)[1])

    def s_copy(d):
        return remote(ss, ssrx.at[d - 1], s_send.at[d - 1], s_recv.at[d - 1], line(d))

    for d in range(1, 8):
        v_copy(d).start()
    total = vs[pl.ds(me_e * vrows, vrows), :]
    for d in range(1, 8):
        v_copy(d).wait_recv()
        total = total + vrx[d - 1]
    vfull[pl.ds(me_e * vrows, vrows), :] = total * (1.0 / rank)
    for d in range(1, 8):
        f_copy(d).start()
    for d in range(1, 8):
        f_landed(d).wait_recv()
    vnew = vfull[...]
    ss[...] = jnp.sum((vnew * vnew).reshape(rows_i // 8, 8, rank), axis=0)
    for d in range(1, nx):
        s_copy(d).start()
    square = ss[...]
    for d in range(1, nx):
        s_copy(d).wait_recv()
        square = square + ssrx[d - 1]
    square = jnp.sum(jnp.sum(square, axis=0, keepdims=True), axis=1, keepdims=True)
    out_ref[...] = vnew * lax.rsqrt(square / (order * rank) + 1e-06)

    def sent(t, carry):
        p_copy(t).wait_send()
        x_copy(t).wait_send()
        y_copy(t).wait_send()
        return carry

    lax.fori_loop(0, steps, sent, 0)
    for k in range(PIECES):
        c_copy(k).wait_send()
        l2_copy(k).wait_send()
        g_copy(k).wait_send()

        @pl.when(has_out)
        def _():
            o_copy(k).wait_send()
    for d in range(1, 8):
        v_copy(d).wait_send()
        f_copy(d).wait_send()
    for d in range(1, nx):
        s_copy(d).wait_send()


def fused(nx, moment, factor_start):
    rows_i, rows_j, rows_k = moment.shape
    order, rank = factor_start.shape
    steps = rows_i // STEP_ROWS
    half, part, piece = rank // 2, rank // 8, rank // 64
    vrows = rows_i // 8
    vmem, dma = pltpu.VMEM, pltpu.SemaphoreType.DMA
    scratch = [
        vmem((MBUFS, STEP_ROWS, rows_j, rows_k), BF16),
        vmem((rank, rows_k), BF16),
        vmem((rank, rows_k), BF16),
        vmem((rank, rows_i), BF16),
        vmem((steps, STEP_ROWS, half, rank), F32),
        vmem((steps, STEP_ROWS, half, rank), BF16),
        vmem((steps, STEP_ROWS, half, rank), BF16),
        vmem((steps, STEP_ROWS, part, rank), BF16),
        vmem((steps, STEP_ROWS, part, rank), BF16),
        vmem((steps, STEP_ROWS, part, rank), BF16),
        vmem((steps, STEP_ROWS, part, rank), BF16),
        vmem((2 * part * rows_i, rank), F32),
        vmem((PIECES, piece, rank, rank), BF16),
        vmem((PIECES, piece, rank, rank), BF16),
        vmem((PIECES, piece, rank, rank), F32),
        vmem((PIECES, piece, rank, rank), BF16),
        vmem((PIECES, piece, rank, rank), BF16),
        vmem((PIECES, piece, rank, rank), BF16),
        vmem((2 * part, rank, rank), BF16),
        vmem((rows_i, rank), F32),
        vmem((7, vrows, rank), F32),
        vmem((rows_i, rank), F32),
        vmem((8, rank), F32),
        vmem((nx - 1, 8, rank), F32),
        dma((MBUFS,)),
        dma((steps,)), dma((steps,)), dma((steps,)), dma((steps,)), dma((steps,)), dma((steps,)),
        dma((PIECES,)), dma((PIECES,)), dma((PIECES,)), dma((PIECES,)), dma((PIECES,)),
        dma((PIECES,)), dma((PIECES,)), dma((PIECES,)),
        dma((7,)), dma((7,)), dma((7,)), dma((7,)),
        dma((nx - 1,)), dma((nx - 1,)),
    ]
    return pl.pallas_call(
        functools.partial(sweep_kernel, nx, order),
        out_shape=jax.ShapeDtypeStruct((rows_i, rank), F32),
        in_specs=[pl.BlockSpec(memory_space=pl.ANY), pl.BlockSpec(memory_space=pltpu.VMEM)],
        out_specs=pl.BlockSpec(memory_space=pltpu.VMEM),
        scratch_shapes=scratch,
        compiler_params=pltpu.CompilerParams(collective_id=0, has_side_effects=True,
                                             vmem_limit_bytes=60 * 1024 * 1024),
        cost_estimate=pl.CostEstimate(flops=2 * rows_i * rows_j * rank * (rows_k + rank),
                                      bytes_accessed=2 * rows_i * rows_j * rows_k, transcendentals=0),
    )(moment, factor_start)


def plain(moment, factor_start):
    rows_i, rows_j, rows_k = moment.shape
    order, rank = factor_start.shape
    scale = 1.0 / order**0.5
    krows = lax.dynamic_slice_in_dim(factor_start, lax.axis_index("gz") * rows_k, rows_k, 0)
    jrows = lax.dynamic_slice_in_dim(factor_start, lax.axis_index("gy") * rows_j, rows_j, 0)
    irows = lax.dynamic_slice_in_dim(factor_start, lax.axis_index("gx") * rows_i, rows_i, 0)
    y = jnp.einsum("ijk,kb->ijb", moment, krows, preferred_element_type=F32).astype(BF16)
    z = jnp.einsum("ijb,ja->iba", y, jrows, preferred_element_type=F32) * scale
    z = lax.psum_scatter(z, "gz", scatter_dimension=1, tiled=True)
    z = lax.psum_scatter(z, "gy", scatter_dimension=2, tiled=True).astype(BF16)
    c = lax.psum(jnp.einsum("iba,ir->bar", z, irows, preferred_element_type=F32), "gx")
    c = (c * scale).astype(BF16)
    v = lax.psum(jnp.einsum("iba,bar->ir", z, c, preferred_element_type=F32), ("gy", "gz")) / rank
    total = lax.psum(jnp.sum(v * v), "gx")
    return v * lax.rsqrt(total / (order * rank) + 1e-06)


def solution(mesh):
    nx, ny, nz = mesh.shape["gx"], mesh.shape["gy"], mesh.shape["gz"]

    def local(moment, factor_start):
        rows_i, rank = moment.shape[0], factor_start.shape[1]
        if ny == 4 and nz == 2 and nx % 2 == 0 and rank == 128 and rows_i % 128 == 0:
            return fused(nx, moment, factor_start)
        return plain(moment, factor_start)

    return jax.shard_map(local, mesh=mesh, in_specs=(P("gx", "gy", "gz"), P()), out_specs=P("gx", None),
                         check_vma=False)
```

```python
import functools

import jax
import jax.numpy as jnp
from jax import lax
from jax.experimental import pallas as pl
from jax.experimental.pallas import tpu as pltpu
from jax.sharding import PartitionSpec as P

MESH = pl.DeviceIdType.MESH
F32 = jnp.float32
BF16 = jnp.bfloat16
STEP_ROWS = 16
MBUFS = 4
PIECES = 8
LAG = 2
AHEAD = 2


def sweep_kernel(nx, order, m_hbm, u_ref, out_ref, mbuf, y_even, y_odd, vs_t, uj_t, ui_t, zown, zsend, prx, xs, ys, rxx, rxy, zz,
                 cs, crx, cown, lsend, r1, r2, cfull, vs, vrx, vfull, ss, ssrx,
                 m_sem, p_send, p_recv, x_send, x_recv, y_send, y_recv, c_send, c_recv, l_send, r1_recv, r2_recv,
                 o_send, g_send, g_recv, v_send, v_recv, f_send, f_recv, s_send, s_recv):
    rows_i, rows_j, rows_k = m_hbm.shape
    rank = u_ref.shape[1]
    steps = rows_i // STEP_ROWS
    scale = 1.0 / order**0.5
    me_x, me_y, me_c = lax.axis_index("gx"), lax.axis_index("gy"), lax.axis_index("gz")
    bit_x, bit_y = lax.rem(me_y, 2), lax.div(me_y, 2)
    at_x = (me_x, me_y + 1 - 2 * bit_x, me_c)
    at_y = (me_x, me_y + 2 - 4 * bit_y, me_c)
    at_c = (me_x, me_y, 1 - me_c)
    me_e = me_y * 2 + me_c
    half = rank // 2
    quarter = rank // 4
    part = rank // 8
    sub = rank // 16
    piece = 2 * sub // PIECES

    def group(d):
        e = lax.rem(me_e + d, 8)
        return e, (me_x, lax.div(e, 2), lax.rem(e, 2))

    def line(d):
        return (lax.rem(me_x + d, nx), me_y, me_c)

    def m_copy(t):
        slot = lax.rem(t, MBUFS)
        return pltpu.make_async_copy(m_hbm.at[pl.ds(t * STEP_ROWS, STEP_ROWS)], mbuf.at[slot], m_sem.at[slot])

    def remote(src, dst, send, recv, to):
        return pltpu.make_async_remote_copy(src_ref=src, dst_ref=dst, send_sem=send, recv_sem=recv,
                                            device_id=to, device_id_type=MESH)

    for t in range(MBUFS - 1):
        m_copy(t).start()

    barrier = pltpu.get_barrier_semaphore()
    for d in range(1, 8):
        pl.semaphore_signal(barrier, inc=1, device_id=group(d)[1], device_id_type=MESH)
    for d in range(1, nx):
        pl.semaphore_signal(barrier, inc=1, device_id=line(d), device_id_type=MESH)

    uj = u_ref[pl.ds(me_y * rows_j, rows_j), :].astype(F32).T
    vs_t[...] = uj.astype(BF16)
    for n, core in enumerate((me_c, 1 - me_c)):
        for m, first in enumerate((bit_x * part, quarter + bit_y * part,
                                   (1 - bit_x) * part, quarter + (1 - bit_y) * part)):
            uj_t[pl.ds(n * half + m * part, part), :] = vs_t[pl.ds(core * half + first, part), :]
    ui_t[...] = u_ref[pl.ds(me_x * rows_i, rows_i), :].astype(F32).T.astype(BF16)
    pl.semaphore_wait(barrier, 7 + nx - 1)

    def p_copy(t):
        return remote(zsend.at[t], prx.at[t], p_send.at[t], p_recv.at[t], at_c)

    def x_copy(t):
        return remote(xs.at[t], rxx.at[t], x_send.at[t], x_recv.at[t], at_x)

    def y_copy(t):
        return remote(ys.at[t], rxy.at[t], y_send.at[t], y_recv.at[t], at_y)

    def first_product(t, y_ref):
        uk = u_ref[pl.ds(me_c * rows_k, rows_k), :]
        slot = lax.rem(t, MBUFS)
        for i in range(0, STEP_ROWS, 4):
            block = mbuf[slot, pl.ds(i, 4)].reshape(4 * rows_j, rows_k)
            y = jnp.dot(block, uk, preferred_element_type=F32)
            y_ref[pl.ds(i * rows_j, 4 * rows_j), :] = y.astype(BF16)

    def second_product(t, y_ref):
        for i in range(0, STEP_ROWS, 4):
            wide = jnp.concatenate([y_ref[pl.ds((i + n) * rows_j, rows_j), :] for n in range(4)], axis=1)
            z = jnp.dot(uj_t[...], wide, preferred_element_type=F32) * scale
            for n in range(4):
                zown[t, i + n] = z[:half, n * rank:(n + 1) * rank]
                zsend[t, i + n] = z[half:, n * rank:(n + 1) * rank].astype(BF16)

    def pair_sum(t):
        xs[t] = (zown[t, :, pl.ds(2 * part, part)] + prx[t, :, pl.ds(2 * part, part)].astype(F32)).astype(BF16)
        ys[t] = (zown[t, :, pl.ds(3 * part, part)] + prx[t, :, pl.ds(3 * part, part)].astype(F32)).astype(BF16)

    def land(t):
        for i in range(STEP_ROWS):
            both = zown[t, i, pl.ds(0, 2 * part)] + prx[t, i, pl.ds(0, 2 * part)].astype(F32)
            far = jnp.concatenate([rxx[t, i], rxy[t, i]], axis=0).astype(F32)
            zz[pl.ds(t * STEP_ROWS + i, 2 * part, stride=rows_i), :] = both + far

    def await_far(t):
        x_copy(t).wait_recv()
        y_copy(t).wait_recv()

    def send_far(t):
        x_copy(t).start()
        y_copy(t).start()

    def step(t, y_old, y_new, sums, lands):
        @pl.when(t + MBUFS - 2 < steps)
        def _():
            m_copy(t + MBUFS - 2).start()

        if sums:
            p_copy(t - 2).wait_recv()
        if lands:
            await_far(t - 2 - LAG)
        m_copy(t).wait()
        if sums:
            pair_sum(t - 2)
            send_far(t - 2)
        if lands:
            land(t - 2 - LAG)
        second_product(t - 1, y_old)
        first_product(t, y_new)
        p_copy(t - 1).start()

    m_copy(0).wait()
    first_product(0, y_even)
    for t in range(1, 2 + LAG):
        old, new = (y_even, y_odd) if t % 2 else (y_odd, y_even)
        step(t, old, new, t >= 2, False)

    def body(n, carry):
        step(2 * n, y_odd, y_even, True, True)
        step(2 * n + 1, y_even, y_odd, True, True)
        return carry

    lax.fori_loop((2 + LAG) // 2, steps // 2, body, 0)
    second_product(steps - 1, y_odd)
    p_copy(steps - 1).start()
    for t in (steps - 2, steps - 1):
        p_copy(t).wait_recv()
        pair_sum(t)
        send_far(t)

    def late(t, carry):
        await_far(t)
        land(t)
        return carry

    lax.fori_loop(steps - 2 - LAG, steps, late, 0)

    def first_of(k, mine):
        if k % 2 == 0:
            bit = bit_y if mine else 1 - bit_y
            return bit * sub + (k // 2) * piece
        bit = bit_x if mine else 1 - bit_x
        return part + bit * sub + (k // 2) * piece

    def wide_z(first):
        return jnp.concatenate([zz[pl.ds((first + n) * rows_i, rows_i), :].astype(BF16) for n in range(piece)], axis=1)

    def core_part(first):
        return jnp.dot(ui_t[...], wide_z(first), preferred_element_type=F32) * scale

    def c_copy(k):
        return remote(cs.at[k], crx.at[k], c_send.at[k], c_recv.at[k], at_y if k % 2 == 0 else at_x)

    for k in range(PIECES):
        c = core_part(first_of(k, False))
        for n in range(piece):
            cs[k, n] = c[:, n * rank:(n + 1) * rank].astype(BF16)
        c_copy(k).start()
    mid = nx // 2
    side = lax.div(me_x, mid)
    inward = (me_x + 1 - 2 * side, me_y, me_c)
    outward = (me_x - 1 + 2 * side, me_y, me_c)
    inner = jnp.logical_or(me_x == mid - 1, me_x == mid)
    has_out = jnp.logical_and(me_x > 0, me_x < nx - 1)
    not_inner = jnp.logical_not(inner)

    def l1_copy(k):
        return remote(lsend.at[k], r1.at[k], l_send.at[k], r1_recv.at[k], inward)

    def l2_copy(k):
        return remote(lsend.at[k], r2.at[k], l_send.at[k], r2_recv.at[k], inward)

    def o_copy(k):
        return remote(cfull.at[pl.ds(first_of(k, True), piece)], r2.at[k], o_send.at[k], r2_recv.at[k], outward)

    def g_copy(k):
        here = cfull.at[pl.ds(first_of(k, True), piece)]
        return remote(here, here, g_send.at[k], g_recv.at[k], at_y if k % 2 == 0 else at_x)

    def g_landed(k):
        here = cfull.at[pl.ds(first_of(k, False), piece)]
        return remote(here, here, g_send.at[k], g_recv.at[k], at_y if k % 2 == 0 else at_x)

    def own_sum(k):
        c = core_part(first_of(k, True))
        c_copy(k).wait_recv()
        for n in range(piece):
            cown[k, n] = c[:, n * rank:(n + 1) * rank] + crx[k, n].astype(F32)

    def add_outer(k):
        @pl.when(has_out)
        def _():
            l1_copy(k).wait_recv()
            cown[k] = cown[k] + r1[k].astype(F32)

        lsend[k] = cown[k].astype(BF16)

    def v_part(first):
        c = jnp.concatenate([cfull[first + n] for n in range(piece)], axis=1)
        return lax.dot_general(wide_z(first), c, (((1,), (1,)), ((), ())), preferred_element_type=F32)

    def send_back(k):
        @pl.when(has_out)
        def _():
            o_copy(k).start()

        g_copy(k).start()

    def add_v(k):
        part_v = v_part(first_of(k, True))
        vs[...] = part_v if k == 0 else vs[...] + part_v

    @pl.when(not_inner)
    def _():
        for k in range(PIECES):
            own_sum(k)
            add_outer(k)
            l1_copy(k).start()
        for k in range(PIECES):
            l2_copy(k).wait_recv()
            cfull[pl.ds(first_of(k, True), piece)] = r2[k]
            send_back(k)
            add_v(k)

    @pl.when(inner)
    def _():
        for k in range(PIECES + AHEAD):
            if k < PIECES:
                own_sum(k)
                add_outer(k)
                l2_copy(k).start()
            if k >= AHEAD:
                n = k - AHEAD
                l2_copy(n).wait_recv()
                cfull[pl.ds(first_of(n, True), piece)] = (lsend[n].astype(F32) + r2[n].astype(F32)).astype(BF16)
                send_back(n)
                add_v(n)

    for k in range(PIECES):
        g_landed(k).wait_recv()
        vs[...] = vs[...] + v_part(first_of(k, False))

    vrows = rows_i // 8

    def v_copy(d):
        e, to = group(d)
        return remote(vs.at[pl.ds(e * vrows, vrows)], vrx.at[d - 1], v_send.at[d - 1], v_recv.at[d - 1], to)

    def f_copy(d):
        here = vfull.at[pl.ds(me_e * vrows, vrows)]
        return remote(here, here, f_send.at[d - 1], f_recv.at[d - 1], group(d)[1])

    def f_landed(d):
        here = vfull.at[pl.ds(group(8 - d)[0] * vrows, vrows)]
        return remote(here, here, f_send.at[d - 1], f_recv.at[d - 1], group(d)[1])

    def s_copy(d):
        return remote(ss, ssrx.at[d - 1], s_send.at[d - 1], s_recv.at[d - 1], line(d))

    for d in range(1, 8):
        v_copy(d).start()
    total = vs[pl.ds(me_e * vrows, vrows), :]
    for d in range(1, 8):
        v_copy(d).wait_recv()
        total = total + vrx[d - 1]
    vfull[pl.ds(me_e * vrows, vrows), :] = total * (1.0 / rank)
    for d in range(1, 8):
        f_copy(d).start()
    for d in range(1, 8):
        f_landed(d).wait_recv()
    vnew = vfull[...]
    ss[...] = jnp.sum((vnew * vnew).reshape(rows_i // 8, 8, rank), axis=0)
    for d in range(1, nx):
        s_copy(d).start()
    square = ss[...]
    for d in range(1, nx):
        s_copy(d).wait_recv()
        square = square + ssrx[d - 1]
    square = jnp.sum(jnp.sum(square, axis=0, keepdims=True), axis=1, keepdims=True)
    out_ref[...] = vnew * lax.rsqrt(square / (order * rank) + 1e-06)

    def sent(t, carry):
        p_copy(t).wait_send()
        x_copy(t).wait_send()
        y_copy(t).wait_send()
        return carry

    lax.fori_loop(0, steps, sent, 0)
    for k in range(PIECES):
        c_copy(k).wait_send()
        l2_copy(k).wait_send()
        g_copy(k).wait_send()

        @pl.when(has_out)
        def _():
            o_copy(k).wait_send()
    for d in range(1, 8):
        v_copy(d).wait_send()
        f_copy(d).wait_send()
    for d in range(1, nx):
        s_copy(d).wait_send()


def fused(nx, moment, factor_start):
    rows_i, rows_j, rows_k = moment.shape
    order, rank = factor_start.shape
    steps = rows_i // STEP_ROWS
    half, part, piece = rank // 2, rank // 8, rank // 64
    vrows = rows_i // 8
    vmem, dma = pltpu.VMEM, pltpu.SemaphoreType.DMA
    scratch = [
        vmem((MBUFS, STEP_ROWS, rows_j, rows_k), BF16),
        vmem((STEP_ROWS * rows_j, rank), BF16),
        vmem((STEP_ROWS * rows_j, rank), BF16),
        vmem((rank, rows_j), BF16),
        vmem((rank, rows_j), BF16),
        vmem((rank, rows_i), BF16),
        vmem((steps, STEP_ROWS, half, rank), F32),
        vmem((steps, STEP_ROWS, half, rank), BF16),
        vmem((steps, STEP_ROWS, half, rank), BF16),
        vmem((steps, STEP_ROWS, part, rank), BF16),
        vmem((steps, STEP_ROWS, part, rank), BF16),
        vmem((steps, STEP_ROWS, part, rank), BF16),
        vmem((steps, STEP_ROWS, part, rank), BF16),
        vmem((2 * part * rows_i, rank), F32),
        vmem((PIECES, piece, rank, rank), BF16),
        vmem((PIECES, piece, rank, rank), BF16),
        vmem((PIECES, piece, rank, rank), F32),
        vmem((PIECES, piece, rank, rank), BF16),
        vmem((PIECES, piece, rank, rank), BF16),
        vmem((PIECES, piece, rank, rank), BF16),
        vmem((2 * part, rank, rank), BF16),
        vmem((rows_i, rank), F32),
        vmem((7, vrows, rank), F32),
        vmem((rows_i, rank), F32),
        vmem((8, rank), F32),
        vmem((nx - 1, 8, rank), F32),
        dma((MBUFS,)),
        dma((steps,)), dma((steps,)), dma((steps,)), dma((steps,)), dma((steps,)), dma((steps,)),
        dma((PIECES,)), dma((PIECES,)), dma((PIECES,)), dma((PIECES,)), dma((PIECES,)),
        dma((PIECES,)), dma((PIECES,)), dma((PIECES,)),
        dma((7,)), dma((7,)), dma((7,)), dma((7,)),
        dma((nx - 1,)), dma((nx - 1,)),
    ]
    return pl.pallas_call(
        functools.partial(sweep_kernel, nx, order),
        out_shape=jax.ShapeDtypeStruct((rows_i, rank), F32),
        in_specs=[pl.BlockSpec(memory_space=pl.ANY), pl.BlockSpec(memory_space=pltpu.VMEM)],
        out_specs=pl.BlockSpec(memory_space=pltpu.VMEM),
        scratch_shapes=scratch,
        compiler_params=pltpu.CompilerParams(collective_id=0, has_side_effects=True,
                                             vmem_limit_bytes=60 * 1024 * 1024),
        cost_estimate=pl.CostEstimate(flops=2 * rows_i * rows_j * rank * (rows_k + rank),
                                      bytes_accessed=2 * rows_i * rows_j * rows_k, transcendentals=0),
    )(moment, factor_start)


def plain(moment, factor_start):
    rows_i, rows_j, rows_k = moment.shape
    order, rank = factor_start.shape
    scale = 1.0 / order**0.5
    krows = lax.dynamic_slice_in_dim(factor_start, lax.axis_index("gz") * rows_k, rows_k, 0)
    jrows = lax.dynamic_slice_in_dim(factor_start, lax.axis_index("gy") * rows_j, rows_j, 0)
    irows = lax.dynamic_slice_in_dim(factor_start, lax.axis_index("gx") * rows_i, rows_i, 0)
    y = jnp.einsum("ijk,kb->ijb", moment, krows, preferred_element_type=F32).astype(BF16)
    z = jnp.einsum("ijb,ja->iba", y, jrows, preferred_element_type=F32) * scale
    z = lax.psum_scatter(z, "gz", scatter_dimension=1, tiled=True)
    z = lax.psum_scatter(z, "gy", scatter_dimension=2, tiled=True).astype(BF16)
    c = lax.psum(jnp.einsum("iba,ir->bar", z, irows, preferred_element_type=F32), "gx")
    c = (c * scale).astype(BF16)
    v = lax.psum(jnp.einsum("iba,bar->ir", z, c, preferred_element_type=F32), ("gy", "gz")) / rank
    total = lax.psum(jnp.sum(v * v), "gx")
    return v * lax.rsqrt(total / (order * rank) + 1e-06)


def solution(mesh):
    nx, ny, nz = mesh.shape["gx"], mesh.shape["gy"], mesh.shape["gz"]

    def local(moment, factor_start):
        rows_i, rank = moment.shape[0], factor_start.shape[1]
        if ny == 4 and nz == 2 and nx % 2 == 0 and rank == 128 and rows_i % 128 == 0:
            return fused(nx, moment, factor_start)
        return plain(moment, factor_start)

    return jax.shard_map(local, mesh=mesh, in_specs=(P("gx", "gy", "gz"), P()), out_specs=P("gx", None),
                         check_vma=False)
```

```python
import functools

import jax
import jax.numpy as jnp
from jax import lax
from jax.experimental import pallas as pl
from jax.experimental.pallas import tpu as pltpu
from jax.sharding import PartitionSpec as P

MESH = pl.DeviceIdType.MESH
F32 = jnp.float32
BF16 = jnp.bfloat16
STEP_ROWS = 16
MBUFS = 4
PIECES = 8
LAG = 2
AHEAD = 2


def sweep_kernel(nx, order, m_hbm, u_ref, out_ref, mbuf, y_even, y_odd, vs_t, uj_t, ui_t, zown, zsend, prx, xs, ys, rxx, rxy, zz,
                 cs, crx, cown, lsend, r1, r2, cfull, vs, vrx, vfull, ss, ssrx,
                 m_sem, p_send, p_recv, x_send, x_recv, y_send, y_recv, c_send, c_recv, l_send, r1_recv, r2_recv,
                 o_send, g_send, g_recv, v_send, v_recv, f_send, f_recv, s_send, s_recv):
    rows_i, rows_j, rows_k = m_hbm.shape
    rank = u_ref.shape[1]
    steps = rows_i // STEP_ROWS
    scale = 1.0 / order**0.5
    me_x, me_y, me_c = lax.axis_index("gx"), lax.axis_index("gy"), lax.axis_index("gz")
    bit_x, bit_y = lax.rem(me_y, 2), lax.div(me_y, 2)
    at_x = (me_x, me_y + 1 - 2 * bit_x, me_c)
    at_y = (me_x, me_y + 2 - 4 * bit_y, me_c)
    at_c = (me_x, me_y, 1 - me_c)
    me_e = me_y * 2 + me_c
    half = rank // 2
    quarter = rank // 4
    part = rank // 8
    sub = rank // 16
    piece = 2 * sub // PIECES

    def group(d):
        e = lax.rem(me_e + d, 8)
        return e, (me_x, lax.div(e, 2), lax.rem(e, 2))

    def line(d):
        return (lax.rem(me_x + d, nx), me_y, me_c)

    def m_copy(t):
        slot = lax.rem(t, MBUFS)
        return pltpu.make_async_copy(m_hbm.at[pl.ds(t * STEP_ROWS, STEP_ROWS)], mbuf.at[slot], m_sem.at[slot])

    def remote(src, dst, send, recv, to):
        return pltpu.make_async_remote_copy(src_ref=src, dst_ref=dst, send_sem=send, recv_sem=recv,
                                            device_id=to, device_id_type=MESH)

    for t in range(MBUFS - 1):
        m_copy(t).start()

    barrier = pltpu.get_barrier_semaphore()
    for d in range(1, 8):
        pl.semaphore_signal(barrier, inc=1, device_id=group(d)[1], device_id_type=MESH)
    for d in range(1, nx):
        pl.semaphore_signal(barrier, inc=1, device_id=line(d), device_id_type=MESH)

    uj = u_ref[pl.ds(me_y * rows_j, rows_j), :].astype(F32).T
    vs_t[...] = uj.astype(BF16)
    for n, core in enumerate((me_c, 1 - me_c)):
        for m, first in enumerate((bit_x * part, quarter + bit_y * part,
                                   (1 - bit_x) * part, quarter + (1 - bit_y) * part)):
            uj_t[pl.ds(n * half + m * part, part), :] = vs_t[pl.ds(core * half + first, part), :]
    ui_t[...] = u_ref[pl.ds(me_x * rows_i, rows_i), :].astype(F32).T.astype(BF16)
    pl.semaphore_wait(barrier, 7 + nx - 1)

    def p_copy(t):
        return remote(zsend.at[t], prx.at[t], p_send.at[t], p_recv.at[t], at_c)

    def x_copy(t):
        return remote(xs.at[t], rxx.at[t], x_send.at[t], x_recv.at[t], at_x)

    def y_copy(t):
        return remote(ys.at[t], rxy.at[t], y_send.at[t], y_recv.at[t], at_y)

    def first_product(t, y_ref):
        uk = u_ref[pl.ds(me_c * rows_k, rows_k), :]
        slot = lax.rem(t, MBUFS)
        block = mbuf[slot].reshape(STEP_ROWS * rows_j, rows_k)
        y_ref[...] = jnp.dot(block, uk, preferred_element_type=F32).astype(BF16)

    def second_product(t, y_ref):
        for i in range(0, STEP_ROWS, 4):
            wide = jnp.concatenate([y_ref[pl.ds((i + n) * rows_j, rows_j), :] for n in range(4)], axis=1)
            z = jnp.dot(uj_t[...], wide, preferred_element_type=F32) * scale
            for n in range(4):
                zown[t, i + n] = z[:half, n * rank:(n + 1) * rank]
                zsend[t, i + n] = z[half:, n * rank:(n + 1) * rank].astype(BF16)

    def pair_sum(t):
        xs[t] = (zown[t, :, pl.ds(2 * part, part)] + prx[t, :, pl.ds(2 * part, part)].astype(F32)).astype(BF16)
        ys[t] = (zown[t, :, pl.ds(3 * part, part)] + prx[t, :, pl.ds(3 * part, part)].astype(F32)).astype(BF16)

    def land(t):
        for i in range(STEP_ROWS):
            both = zown[t, i, pl.ds(0, 2 * part)] + prx[t, i, pl.ds(0, 2 * part)].astype(F32)
            far = jnp.concatenate([rxx[t, i], rxy[t, i]], axis=0).astype(F32)
            zz[pl.ds(t * STEP_ROWS + i, 2 * part, stride=rows_i), :] = both + far

    def await_far(t):
        x_copy(t).wait_recv()
        y_copy(t).wait_recv()

    def send_far(t):
        x_copy(t).start()
        y_copy(t).start()

    def step(t, y_old, y_new, sums, lands):
        @pl.when(t + MBUFS - 2 < steps)
        def _():
            m_copy(t + MBUFS - 2).start()

        if sums:
            p_copy(t - 2).wait_recv()
        if lands:
            await_far(t - 2 - LAG)
        m_copy(t).wait()
        if sums:
            pair_sum(t - 2)
            send_far(t - 2)
        if lands:
            land(t - 2 - LAG)
        second_product(t - 1, y_old)
        first_product(t, y_new)
        p_copy(t - 1).start()

    m_copy(0).wait()
    first_product(0, y_even)
    for t in range(1, 2 + LAG):
        old, new = (y_even, y_odd) if t % 2 else (y_odd, y_even)
        step(t, old, new, t >= 2, False)

    def body(n, carry):
        step(2 * n, y_odd, y_even, True, True)
        step(2 * n + 1, y_even, y_odd, True, True)
        return carry

    lax.fori_loop((2 + LAG) // 2, steps // 2, body, 0)
    second_product(steps - 1, y_odd)
    p_copy(steps - 1).start()
    for t in (steps - 2, steps - 1):
        p_copy(t).wait_recv()
        pair_sum(t)
        send_far(t)

    def late(t, carry):
        await_far(t)
        land(t)
        return carry

    lax.fori_loop(steps - 2 - LAG, steps, late, 0)

    def first_of(k, mine):
        if k % 2 == 0:
            bit = bit_y if mine else 1 - bit_y
            return bit * sub + (k // 2) * piece
        bit = bit_x if mine else 1 - bit_x
        return part + bit * sub + (k // 2) * piece

    def wide_z(first):
        return jnp.concatenate([zz[pl.ds((first + n) * rows_i, rows_i), :].astype(BF16) for n in range(piece)], axis=1)

    def core_part(first):
        return jnp.dot(ui_t[...], wide_z(first), preferred_element_type=F32) * scale

    def c_copy(k):
        return remote(cs.at[k], crx.at[k], c_send.at[k], c_recv.at[k], at_y if k % 2 == 0 else at_x)

    for k in range(PIECES):
        c = core_part(first_of(k, False))
        for n in range(piece):
            cs[k, n] = c[:, n * rank:(n + 1) * rank].astype(BF16)
        c_copy(k).start()
    mid = nx // 2
    side = lax.div(me_x, mid)
    inward = (me_x + 1 - 2 * side, me_y, me_c)
    outward = (me_x - 1 + 2 * side, me_y, me_c)
    inner = jnp.logical_or(me_x == mid - 1, me_x == mid)
    has_out = jnp.logical_and(me_x > 0, me_x < nx - 1)
    not_inner = jnp.logical_not(inner)

    def l1_copy(k):
        return remote(lsend.at[k], r1.at[k], l_send.at[k], r1_recv.at[k], inward)

    def l2_copy(k):
        return remote(lsend.at[k], r2.at[k], l_send.at[k], r2_recv.at[k], inward)

    def o_copy(k):
        return remote(cfull.at[pl.ds(first_of(k, True), piece)], r2.at[k], o_send.at[k], r2_recv.at[k], outward)

    def g_copy(k):
        here = cfull.at[pl.ds(first_of(k, True), piece)]
        return remote(here, here, g_send.at[k], g_recv.at[k], at_y if k % 2 == 0 else at_x)

    def g_landed(k):
        here = cfull.at[pl.ds(first_of(k, False), piece)]
        return remote(here, here, g_send.at[k], g_recv.at[k], at_y if k % 2 == 0 else at_x)

    def own_sum(k):
        c = core_part(first_of(k, True))
        c_copy(k).wait_recv()
        for n in range(piece):
            cown[k, n] = c[:, n * rank:(n + 1) * rank] + crx[k, n].astype(F32)

    def add_outer(k):
        @pl.when(has_out)
        def _():
            l1_copy(k).wait_recv()
            cown[k] = cown[k] + r1[k].astype(F32)

        lsend[k] = cown[k].astype(BF16)

    def v_part(first):
        c = jnp.concatenate([cfull[first + n] for n in range(piece)], axis=1)
        return lax.dot_general(wide_z(first), c, (((1,), (1,)), ((), ())), preferred_element_type=F32)

    def send_back(k):
        @pl.when(has_out)
        def _():
            o_copy(k).start()

        g_copy(k).start()

    def add_v(k):
        part_v = v_part(first_of(k, True))
        vs[...] = part_v if k == 0 else vs[...] + part_v

    @pl.when(not_inner)
    def _():
        for k in range(PIECES):
            own_sum(k)
            add_outer(k)
            l1_copy(k).start()
        for k in range(PIECES):
            l2_copy(k).wait_recv()
            cfull[pl.ds(first_of(k, True), piece)] = r2[k]
            send_back(k)
            add_v(k)

    @pl.when(inner)
    def _():
        for k in range(PIECES + AHEAD):
            if k < PIECES:
                own_sum(k)
                add_outer(k)
                l2_copy(k).start()
            if k >= AHEAD:
                n = k - AHEAD
                l2_copy(n).wait_recv()
                cfull[pl.ds(first_of(n, True), piece)] = (lsend[n].astype(F32) + r2[n].astype(F32)).astype(BF16)
                send_back(n)
                add_v(n)

    for k in range(PIECES):
        g_landed(k).wait_recv()
        vs[...] = vs[...] + v_part(first_of(k, False))

    vrows = rows_i // 8

    def v_copy(d):
        e, to = group(d)
        return remote(vs.at[pl.ds(e * vrows, vrows)], vrx.at[d - 1], v_send.at[d - 1], v_recv.at[d - 1], to)

    def f_copy(d):
        here = vfull.at[pl.ds(me_e * vrows, vrows)]
        return remote(here, here, f_send.at[d - 1], f_recv.at[d - 1], group(d)[1])

    def f_landed(d):
        here = vfull.at[pl.ds(group(8 - d)[0] * vrows, vrows)]
        return remote(here, here, f_send.at[d - 1], f_recv.at[d - 1], group(d)[1])

    def s_copy(d):
        return remote(ss, ssrx.at[d - 1], s_send.at[d - 1], s_recv.at[d - 1], line(d))

    for d in range(1, 8):
        v_copy(d).start()
    total = vs[pl.ds(me_e * vrows, vrows), :]
    for d in range(1, 8):
        v_copy(d).wait_recv()
        total = total + vrx[d - 1]
    vfull[pl.ds(me_e * vrows, vrows), :] = total * (1.0 / rank)
    for d in range(1, 8):
        f_copy(d).start()
    for d in range(1, 8):
        f_landed(d).wait_recv()
    vnew = vfull[...]
    ss[...] = jnp.sum((vnew * vnew).reshape(rows_i // 8, 8, rank), axis=0)
    for d in range(1, nx):
        s_copy(d).start()
    square = ss[...]
    for d in range(1, nx):
        s_copy(d).wait_recv()
        square = square + ssrx[d - 1]
    square = jnp.sum(jnp.sum(square, axis=0, keepdims=True), axis=1, keepdims=True)
    out_ref[...] = vnew * lax.rsqrt(square / (order * rank) + 1e-06)

    def sent(t, carry):
        p_copy(t).wait_send()
        x_copy(t).wait_send()
        y_copy(t).wait_send()
        return carry

    lax.fori_loop(0, steps, sent, 0)
    for k in range(PIECES):
        c_copy(k).wait_send()
        l2_copy(k).wait_send()
        g_copy(k).wait_send()

        @pl.when(has_out)
        def _():
            o_copy(k).wait_send()
    for d in range(1, 8):
        v_copy(d).wait_send()
        f_copy(d).wait_send()
    for d in range(1, nx):
        s_copy(d).wait_send()


def fused(nx, moment, factor_start):
    rows_i, rows_j, rows_k = moment.shape
    order, rank = factor_start.shape
    steps = rows_i // STEP_ROWS
    half, part, piece = rank // 2, rank // 8, rank // 64
    vrows = rows_i // 8
    vmem, dma = pltpu.VMEM, pltpu.SemaphoreType.DMA
    scratch = [
        vmem((MBUFS, STEP_ROWS, rows_j, rows_k), BF16),
        vmem((STEP_ROWS * rows_j, rank), BF16),
        vmem((STEP_ROWS * rows_j, rank), BF16),
        vmem((rank, rows_j), BF16),
        vmem((rank, rows_j), BF16),
        vmem((rank, rows_i), BF16),
        vmem((steps, STEP_ROWS, half, rank), F32),
        vmem((steps, STEP_ROWS, half, rank), BF16),
        vmem((steps, STEP_ROWS, half, rank), BF16),
        vmem((steps, STEP_ROWS, part, rank), BF16),
        vmem((steps, STEP_ROWS, part, rank), BF16),
        vmem((steps, STEP_ROWS, part, rank), BF16),
        vmem((steps, STEP_ROWS, part, rank), BF16),
        vmem((2 * part * rows_i, rank), F32),
        vmem((PIECES, piece, rank, rank), BF16),
        vmem((PIECES, piece, rank, rank), BF16),
        vmem((PIECES, piece, rank, rank), F32),
        vmem((PIECES, piece, rank, rank), BF16),
        vmem((PIECES, piece, rank, rank), BF16),
        vmem((PIECES, piece, rank, rank), BF16),
        vmem((2 * part, rank, rank), BF16),
        vmem((rows_i, rank), F32),
        vmem((7, vrows, rank), F32),
        vmem((rows_i, rank), F32),
        vmem((8, rank), F32),
        vmem((nx - 1, 8, rank), F32),
        dma((MBUFS,)),
        dma((steps,)), dma((steps,)), dma((steps,)), dma((steps,)), dma((steps,)), dma((steps,)),
        dma((PIECES,)), dma((PIECES,)), dma((PIECES,)), dma((PIECES,)), dma((PIECES,)),
        dma((PIECES,)), dma((PIECES,)), dma((PIECES,)),
        dma((7,)), dma((7,)), dma((7,)), dma((7,)),
        dma((nx - 1,)), dma((nx - 1,)),
    ]
    return pl.pallas_call(
        functools.partial(sweep_kernel, nx, order),
        out_shape=jax.ShapeDtypeStruct((rows_i, rank), F32),
        in_specs=[pl.BlockSpec(memory_space=pl.ANY), pl.BlockSpec(memory_space=pltpu.VMEM)],
        out_specs=pl.BlockSpec(memory_space=pltpu.VMEM),
        scratch_shapes=scratch,
        compiler_params=pltpu.CompilerParams(collective_id=0, has_side_effects=True,
                                             vmem_limit_bytes=60 * 1024 * 1024),
        cost_estimate=pl.CostEstimate(flops=2 * rows_i * rows_j * rank * (rows_k + rank),
                                      bytes_accessed=2 * rows_i * rows_j * rows_k, transcendentals=0),
    )(moment, factor_start)


def plain(moment, factor_start):
    rows_i, rows_j, rows_k = moment.shape
    order, rank = factor_start.shape
    scale = 1.0 / order**0.5
    krows = lax.dynamic_slice_in_dim(factor_start, lax.axis_index("gz") * rows_k, rows_k, 0)
    jrows = lax.dynamic_slice_in_dim(factor_start, lax.axis_index("gy") * rows_j, rows_j, 0)
    irows = lax.dynamic_slice_in_dim(factor_start, lax.axis_index("gx") * rows_i, rows_i, 0)
    y = jnp.einsum("ijk,kb->ijb", moment, krows, preferred_element_type=F32).astype(BF16)
    z = jnp.einsum("ijb,ja->iba", y, jrows, preferred_element_type=F32) * scale
    z = lax.psum_scatter(z, "gz", scatter_dimension=1, tiled=True)
    z = lax.psum_scatter(z, "gy", scatter_dimension=2, tiled=True).astype(BF16)
    c = lax.psum(jnp.einsum("iba,ir->bar", z, irows, preferred_element_type=F32), "gx")
    c = (c * scale).astype(BF16)
    v = lax.psum(jnp.einsum("iba,bar->ir", z, c, preferred_element_type=F32), ("gy", "gz")) / rank
    total = lax.psum(jnp.sum(v * v), "gx")
    return v * lax.rsqrt(total / (order * rank) + 1e-06)


def solution(mesh):
    nx, ny, nz = mesh.shape["gx"], mesh.shape["gy"], mesh.shape["gz"]

    def local(moment, factor_start):
        rows_i, rank = moment.shape[0], factor_start.shape[1]
        if ny == 4 and nz == 2 and nx % 2 == 0 and rank == 128 and rows_i % 128 == 0:
            return fused(nx, moment, factor_start)
        return plain(moment, factor_start)

    return jax.shard_map(local, mesh=mesh, in_specs=(P("gx", "gy", "gz"), P()), out_specs=P("gx", None),
                         check_vma=False)
```
